256 devices in a mesh: quad: 4 (over x), box: 64 (over z, y, core).
Axes of the slice: x: 4, y: 4, z: 8, core: 2. Of those that a mesh axis runs over, the one named last changes fastest.
Arguments:
- sample_box: int32 [524288], P(('quad', 'box')), may hold values from -1 to 1023, as said below
- sample_coords: float32 [4, 524288], P(None, ('quad', 'box')), may hold values from -1 to 1
- sample_values: float32 [2, 524288], P(None, ('quad', 'box')), may hold values from -0.6 to 0.6
- level_one: float32 [2, 2, 128, 128], replicated, may hold values from -0.375 to 0.375
- level_two: float32 [2, 2, 128, 128], replicated, may hold values from -0.375 to 0.375
- phase_one: float32 [4, 1024, 64, 512], P('quad', 'box'), may hold values from -3.140625 to 3.140625
- phase_two: float32 [4, 1024, 64, 512], P('quad', 'box'), may hold values from -3.140625 to 3.140625
Outputs:
- image: float32 [4, 1024, 128, 512], P('quad', 'box')
The draws below stay inside these ranges and needn't reach their ends.
Inputs may be any that keep to these rules, and one draw needn't show every extreme that they name: `sample_box`: rows of one device name boxes of that device's quadrant, or -1 for an empty row. Call owner o the boxes o * 16 to (o + 1) * 16 - 1. Among the rows of one device, each owner is named by 15 to 62 rows; one owner, the same for every device of a draw, is named by exactly 62 rows on every device.
All inputs are finite; a program needn't handle non-finite values.
Results may differ from the reference program's by a relative error of at most 0.0003.
Values sent between devices are 32-bit elements; how exact they have to be, the bound alone decides.
No kernel may reach another device: no remote copies, remote signals or barrier semaphores. Data moves between devices by JAX's collectives and lax.ppermute only.
A program may use at most 128 MiB of HBM per device.

```python
import jax
import jax.numpy as jnp
import numpy as np
from jax import lax

RANK = 64
S_DEV = 2048
BOXES_DEV = 16
TGT = 512
CAP = 62
BOXES = 1024
SAMPLES = 524288
N_QUAD = 4
N_BOX = 64


def draw_sample_box(key, part):
    key = jax.random.fold_in(key, 11)
    devices_all = N_QUAD * N_BOX
    key_counts, key_hot, key_order, key_local = jax.random.split(key, 4)
    counts = jax.random.randint(key_counts, (devices_all, N_BOX), CAP // 4, CAP // 2 + 1)
    hot_owner = jax.random.randint(key_hot, (), 0, N_BOX)
    counts = jnp.where(jnp.arange(N_BOX)[None, :] == hot_owner, CAP, counts).astype(jnp.int32)
    ends = jnp.cumsum(counts, axis=1).astype(jnp.int32)
    scores = jax.random.randint(key_order, (devices_all, S_DEV), 0, 2 ** 16) * S_DEV + jnp.arange(S_DEV, dtype=jnp.int32)[None, :]
    positions = jnp.argsort(scores, axis=1, stable=True).astype(jnp.int32)
    owner = jax.vmap(lambda edges, spots: jnp.searchsorted(edges, spots, side='right'))(ends, positions).astype(jnp.int32)
    local_box = jax.random.randint(key_local, (devices_all, S_DEV), 0, BOXES_DEV)
    boxes = jnp.where(owner < N_BOX, owner * BOXES_DEV + local_box, -1).astype(jnp.int32)
    return boxes.reshape(SAMPLES)


def level_of(rng, extent, cuts, least, largest):
    gain = 1.0
    for position, blocks in cuts:
        draws = jax.random.uniform(jax.random.fold_in(jax.random.fold_in(rng, 6), position), (blocks,), jnp.float32, least / len(cuts), largest / len(cuts))
        gain = gain * jnp.repeat(jnp.exp(draws), extent[position] // blocks).reshape((-1,) + (1,) * (len(extent) - 1 - position))
    return gain


def centred(stream_key, extent, spread, limit, cuts=(), held_as=jnp.bfloat16):
    drawn = spread * jax.random.normal(stream_key, extent, jnp.float32)
    if cuts:
        drawn = drawn * level_of(stream_key, extent, cuts, -0.22, 0.18)
    return jnp.clip(drawn, -limit, limit).astype(held_as)


def setup_inputs(seed: int = 0) -> dict:
    seeds = jax.random.split(jax.random.key(seed), 8)
    return {
        "sample_box": draw_sample_box(jax.random.fold_in(seeds[7], 71), 0),
        "sample_coords": jnp.clip(jax.random.uniform(seeds[1], (4, SAMPLES), jnp.float32, -1.0, 1.0) * level_of(seeds[1], (4, SAMPLES), ((1, 256),), -0.4, 0.0), -1.0, 1.0),
        "sample_values": centred(seeds[2], (2, SAMPLES), 0.1, 0.6, ((1, 256),), jnp.float32),
        "level_one": centred(seeds[3], (2, 2, 2 * RANK, 2 * RANK), (4 * RANK) ** -0.5, 0.375, (), jnp.float32),
        "level_two": centred(seeds[4], (2, 2, 2 * RANK, 2 * RANK), (4 * RANK) ** -0.5, 0.375, (), jnp.float32),
        "phase_one": jnp.clip(jax.random.uniform(seeds[5], (N_QUAD, BOXES, RANK, TGT), jnp.float32, -3.140625, 3.140625), -3.140625, 3.140625),
        "phase_two": jnp.clip(jax.random.uniform(seeds[6], (N_QUAD, BOXES, RANK, TGT), jnp.float32, -3.140625, 3.140625), -3.140625, 3.140625),
    }


wavenumber = 6.0


def node_table():
    nodes = np.cos(np.pi * (2.0 * np.arange(8) + 1.0) / 16.0)
    scales = []
    for center in range(8):
        product = 1.0
        for other_node in range(8):
            if other_node != center:
                product = product * (nodes[center] - nodes[other_node])
        scales.append(1.0 / product)
    return [float(v) for v in nodes], scales


def lagrange(points):
    nodes, scales = node_table()
    columns = []
    for center in range(8):
        factor = jnp.full_like(points, scales[center])
        for other_node in range(8):
            if other_node != center:
                factor = factor * (points - nodes[other_node])
        columns.append(factor)
    return jnp.stack(columns, axis=0)


def leaf_block(local_box, coords, values, box_count, targets):
    width = coords.shape[1]
    first_axis = lagrange(coords[0])
    second_axis = lagrange(coords[1])
    basis = (first_axis[:, None, :] * second_axis[None, :, :]).reshape(64, width)
    marks = (local_box[None, :] == jnp.arange(box_count, dtype=jnp.int32)[:, None]).astype(jnp.float32)
    weights = (marks[:, None, :] * basis[None, :, :]).reshape(box_count * 64, width)
    angles = 2.0 * jnp.pi * jnp.arange(targets, dtype=jnp.float32) / targets
    theta = wavenumber * (coords[2][None, :] * jnp.cos(angles)[:, None] + coords[3][None, :] * jnp.sin(angles)[:, None])
    cosine = jnp.cos(theta)
    sine = jnp.sin(theta)
    real_part = values[0][None, :] * cosine - values[1][None, :] * sine
    imag_part = values[0][None, :] * sine + values[1][None, :] * cosine
    dims = (((1,), (1,)), ((), ()))
    real_sum = lax.dot_general(weights, real_part, dims, precision=lax.Precision.HIGHEST)
    imag_sum = lax.dot_general(weights, imag_part, dims, precision=lax.Precision.HIGHEST)
    stacked = jnp.stack([real_sum.reshape(box_count, 64, targets), imag_sum.reshape(box_count, 64, targets)], axis=1)
    return stacked.reshape(box_count, 128, targets)


def apply_matrix(matrix, coef):
    return jnp.einsum('ij,bjt->bit', matrix, coef, precision=lax.Precision.HIGHEST)


def rotate(coef, angle):
    real_part = coef[:, :64]
    imag_part = coef[:, 64:]
    cosine = jnp.cos(angle)
    sine = jnp.sin(angle)
    return jnp.concatenate([cosine * real_part - sine * imag_part, sine * real_part + cosine * imag_part], axis=1)


def evaluate(coef):
    pixels = -1.0 + (2.0 * jnp.arange(8, dtype=jnp.float32) + 1.0) / 8.0
    weights = lagrange(pixels)
    vmatrix = jnp.einsum('ki,mj->ijkm', weights, weights).reshape(64, 64)
    count = coef.shape[0]
    targets = coef.shape[2]
    parts = coef.reshape(count, 2, 64, targets)
    result = jnp.einsum('pj,bcjt->bcpt', vmatrix, parts, precision=lax.Precision.HIGHEST)
    return result.reshape(count, 128, targets)


def reference(sample_box, sample_coords, sample_values, level_one, level_two, phase_one, phase_two):
    devices_all = N_QUAD * N_BOX
    quad_of = (jnp.arange(SAMPLES, dtype=jnp.int32) // S_DEV) // N_BOX
    total_boxes = N_QUAD * BOXES
    sort_key = jnp.where(sample_box >= 0, quad_of * BOXES + sample_box, total_boxes).astype(jnp.int32)
    order = jnp.argsort(sort_key, stable=True)
    rows_max = N_BOX * CAP
    sorted_key = jnp.concatenate([sort_key[order], jnp.full((rows_max,), total_boxes, jnp.int32)])
    sorted_coords = jnp.concatenate([sample_coords[:, order], jnp.zeros((4, rows_max), jnp.float32)], axis=1)
    sorted_values = jnp.concatenate([sample_values[:, order], jnp.zeros((2, rows_max), jnp.float32)], axis=1)
    owners = jnp.arange(devices_all, dtype=jnp.int32)
    starts = jnp.searchsorted(sorted_key, owners * BOXES_DEV, side='left').astype(jnp.int32)

    def one_owner(pair):
        owner, start = pair
        keys = lax.dynamic_slice_in_dim(sorted_key, start, rows_max)
        coords = lax.dynamic_slice_in_dim(sorted_coords, start, rows_max, 1)
        values = lax.dynamic_slice_in_dim(sorted_values, start, rows_max, 1)
        local_box = keys - owner * BOXES_DEV
        inside = (local_box >= 0) & (local_box < BOXES_DEV)
        local_box = jnp.where(inside, local_box, -1).astype(jnp.int32)
        values = jnp.where(inside[None, :], values, jnp.zeros_like(values))
        return leaf_block(local_box, coords, values, BOXES_DEV, TGT)

    leaves = lax.map(one_owner, (owners, starts)).reshape(N_QUAD, BOXES, 128, TGT)
    first_level = []
    for quad_index in range(4):
        low_bit = quad_index % 2
        base = quad_index - low_bit
        summed = apply_matrix(level_one[0, low_bit], leaves[base]) + apply_matrix(level_one[1, low_bit], leaves[base + 1])
        first_level.append(rotate(summed, phase_one[quad_index]))
    images = []
    for quad_index in range(4):
        high_bit = quad_index // 2
        base = quad_index % 2
        summed = apply_matrix(level_two[0, high_bit], first_level[base]) + apply_matrix(level_two[1, high_bit], first_level[base + 2])
        images.append(evaluate(rotate(summed, phase_two[quad_index])))
    return jnp.stack(images, axis=0)
```

```python
import functools

import jax
import jax.numpy as jnp
import numpy as np
from jax import lax
from jax.experimental import pallas as pl
from jax.experimental.pallas import tpu as pltpu
from jax.sharding import PartitionSpec as P

WAVENUMBER = 6.0
SLOTS = 64
TILE = 256
VMEM_LIMIT = 56 * 1024 * 1024

F32 = jnp.float32
BF16 = jnp.bfloat16
NN = (((1,), (0,)), ((), ()))
NT = (((1,), (1,)), ((), ()))


def node_table():
    nodes = np.cos(np.pi * (2.0 * np.arange(8) + 1.0) / 16.0)
    scales = []
    for center in range(8):
        product = 1.0
        for other_node in range(8):
            if other_node != center:
                product = product * (nodes[center] - nodes[other_node])
        scales.append(1.0 / product)
    return ([float(v) for v in nodes], scales)


def lagrange_row(points, center):
    nodes, scales = node_table()
    factor = None
    for other_node in range(8):
        if other_node != center:
            term = points - nodes[other_node]
            factor = term if factor is None else factor * term
    return factor * scales[center]


def pixel_matrix():
    nodes, scales = node_table()
    pixels = -1.0 + (2.0 * np.arange(8) + 1.0) / 8.0
    weights = np.zeros((8, 8))
    for center in range(8):
        value = np.full(8, scales[center])
        for other_node in range(8):
            if other_node != center:
                value = value * (pixels - nodes[other_node])
        weights[center] = value
    one_part = np.einsum("ki,mj->ijkm", weights, weights).reshape(64, 64)
    return np.kron(np.eye(2), one_part).astype(np.float32)


def series(function, limit, terms):
    grid = 0.5 * limit * limit * (1.0 - np.cos(np.pi * (np.arange(400) + 0.5) / 400))
    values = function(np.sqrt(grid))
    fit = np.polynomial.chebyshev.Chebyshev.fit(grid, values, terms - 1, domain=[0, limit * limit])
    return [float(v) for v in fit.convert(kind=np.polynomial.Polynomial).coef]


def horner(coefs, square):
    total = coefs[-1]
    for coef in coefs[-2::-1]:
        total = total * square + coef
    return total


def cos_sin(small, doublings, limit, sin_terms, cos_terms):
    square = small * small
    sine = horner(series(lambda x: np.sinc(x / np.pi), limit, sin_terms), square) * small
    cosine = horner(series(np.cos, limit, cos_terms), square)
    for _ in range(doublings):
        twice = sine + sine
        cosine, sine = 1.0 - twice * sine, twice * cosine
    return cosine, sine


def split_two(value):
    high = value.astype(BF16)
    return high, (value - high.astype(F32)).astype(BF16)


def split_three(value):
    high = value.astype(BF16)
    rest = value - high.astype(F32)
    middle = rest.astype(BF16)
    low = (rest - middle.astype(F32)).astype(BF16)
    return high, middle, low


def product(left, right, dims=NN):
    left_high, left_low = split_two(left)
    right_high, right_low = split_two(right)
    dot = functools.partial(lax.dot_general, dimension_numbers=dims, preferred_element_type=F32)
    return dot(left_high, right_high) + (dot(left_low, right_high) + dot(left_high, right_low))


def strict_upper(size):
    rows = lax.broadcasted_iota(jnp.int32, (size, size), 0)
    columns = lax.broadcasted_iota(jnp.int32, (size, size), 1)
    return jnp.where(rows < columns, 1.0, 0.0).astype(BF16)


def pack_kernel(box_ref, coords_ref, values_ref, out_ref):
    owners = out_ref.shape[0] // 4
    rows = box_ref.shape[1]
    tri = strict_upper(256)
    owner_ids = lax.broadcasted_iota(jnp.int32, (owners, 256), 0)
    row_owner = lax.broadcasted_iota(jnp.int32, (owners * 4, 256), 0) >> 2
    slot_ids = lax.broadcasted_iota(jnp.int32, (2 * SLOTS, 256), 0)
    carry = jnp.zeros((owners, 1), F32)
    total = jnp.zeros((owners * 4, 2 * SLOTS), F32)
    for start in range(0, rows, 256):
        box = box_ref[:, start : start + 256]
        owner = box >> 4
        mark = jnp.where(owner_ids == owner, 1.0, 0.0)
        ahead = lax.dot_general(mark.astype(BF16), tri, NN, preferred_element_type=F32) + carry
        carry = carry + jnp.sum(mark, axis=1, keepdims=True)
        slot = jnp.sum(mark * ahead, axis=0, keepdims=True).astype(jnp.int32)
        key = ((box & 15) + 1).astype(F32)
        coords = coords_ref[:, start : start + 256]
        values = values_ref[:, start : start + 256]
        empty = jnp.zeros_like(key)
        low_fields = jnp.concatenate([key, coords[0:3]], axis=0)
        high_fields = jnp.concatenate([coords[3:4], values, empty], axis=0)
        hit = row_owner == owner
        for fields, shift in ((low_fields, 0), (high_fields, SLOTS)):
            place = jnp.where(slot_ids == slot + shift, 1.0, 0.0).astype(BF16)
            twice = jnp.concatenate([fields, fields], axis=0)
            spread = jnp.broadcast_to(twice[None], (owners // 2, 8, 256)).reshape(owners * 4, 256)
            for part in split_three(jnp.where(hit, spread, 0.0)):
                total = total + lax.dot_general(part, place, NT, preferred_element_type=F32)
    out_ref[...] = total


def sort_kernel(in_ref, out_ref, fields_ref):
    senders = in_ref.shape[0] // 4
    tiles = senders * SLOTS // 128
    lane = lax.broadcasted_iota(jnp.int32, (4, 128), 1)
    for pair in range(senders // 2):
        first = in_ref[8 * pair : 8 * pair + 4, :]
        second = in_ref[8 * pair + 4 : 8 * pair + 8, :]
        low = jnp.where(lane < SLOTS, first, pltpu.roll(second, SLOTS, 1))
        high = jnp.where(lane < SLOTS, pltpu.roll(first, SLOTS, 1), second)
        fields_ref[:, 128 * pair : 128 * (pair + 1)] = jnp.concatenate([low, high], axis=0)
    width = tiles * 128
    tri = strict_upper(256)
    ids = lax.broadcasted_iota(jnp.int32, (16, 256), 0) + 1
    base = jnp.zeros((16, 1), F32)
    count = jnp.zeros((1, 1), F32)
    for start in range(0, width, 256):
        key = fields_ref[0:1, start : start + 256].astype(jnp.int32)
        below = (key >= 1) & (key < ids)
        base = base + jnp.sum(jnp.where(below, 1.0, 0.0), axis=1, keepdims=True)
        count = count + jnp.sum(jnp.where(key >= 1, 1.0, 0.0), axis=1, keepdims=True)
    tile_ids = lax.broadcasted_iota(jnp.int32, (tiles * 8, 256), 0) >> 3
    lane_ids = lax.broadcasted_iota(jnp.int32, (128, 256), 0)
    carry = base
    total = jnp.zeros((tiles * 8, 128), F32)
    for start in range(0, width, 256):
        fields = fields_ref[:, start : start + 256]
        key = fields[0:1].astype(jnp.int32)
        mark = jnp.where(key == ids, 1.0, 0.0)
        ahead = lax.dot_general(mark.astype(BF16), tri, NN, preferred_element_type=F32) + carry
        carry = carry + jnp.sum(mark, axis=1, keepdims=True)
        spot = jnp.sum(mark * ahead, axis=0, keepdims=True).astype(jnp.int32)
        spot = jnp.where(key >= 1, spot, -1)
        hit = tile_ids == (spot >> 7)
        place = jnp.where(lane_ids == (spot & 127), 1.0, 0.0).astype(BF16)
        spread = jnp.broadcast_to(fields[None], (tiles, 8, 256)).reshape(tiles * 8, 256)
        for part in split_three(jnp.where(hit, spread, 0.0)):
            total = total + lax.dot_general(part, place, NT, preferred_element_type=F32)
    out_ref[0:tiles] = total.reshape(tiles, 8, 128)
    out_ref[tiles] = jnp.broadcast_to(base[0:8], (8, 128))
    out_ref[tiles + 1] = jnp.broadcast_to(base[8:16], (8, 128))
    out_ref[tiles + 2] = jnp.broadcast_to(count, (8, 128))


def leaf_kernel(
    info_ref, s0_ref, s1_ref, s2_ref, s3_ref, circle_ref, one_ref, two_ref, phase_ref,
    partner_ref, own_ref, fields_ref, wave_ref, weight_ref, leaf_ref, state_ref,
):
    box = pl.program_id(0)
    tiles = s0_ref.shape[0] - 3

    @pl.when(box == 0)
    def _():
        for index, ref in enumerate((s0_ref, s1_ref, s2_ref, s3_ref)):
            for tile in range(tiles):
                fields_ref[index, tile // 2, :, 128 * (tile % 2) : 128 * (tile % 2 + 1)] = ref[tile]
            state_ref[index] = -1

    @pl.loop(0, 4)
    def _(index):
        start = info_ref[index, box]
        stop = info_ref[index, box + 1]
        leaf_ref[index] = jnp.zeros_like(leaf_ref[index])

        @pl.loop(start // TILE, (stop + TILE - 1) // TILE)
        def _(tile):
            @pl.when(state_ref[index] != tile)
            def _():
                state_ref[index] = tile
                fields = fields_ref[index, tile]
                for half in range(2):
                    columns = slice(128 * half, 128 * (half + 1))
                    first = fields[3:4, columns]
                    second = fields[4:5, columns]
                    for row in range(0, 256, 32):
                        small = (
                            circle_ref[0, row : row + 32] * first
                            + circle_ref[1, row : row + 32] * second
                        )
                        cosine, sine = cos_sin(small, 3, 1.0608, 4, 5)
                        for part, value in ((0, cosine), (256, sine)):
                            high, low = split_two(value)
                            wave_ref[index, 0, part + row : part + row + 32, columns] = high
                            wave_ref[index, 1, part + row : part + row + 32, columns] = low
                first_axis = [lagrange_row(fields[1:2], k) for k in range(8)]
                second_axis = jnp.concatenate(
                    [lagrange_row(fields[2:3], k) for k in range(8)], axis=0
                )
                for part in range(2):
                    scaled = second_axis * fields[5 + part : 6 + part]
                    weights = jnp.concatenate([first_axis[k] * scaled for k in range(8)], axis=0)
                    high, low = split_two(weights)
                    weight_ref[index, 64 * part : 64 * part + 64] = high
                    weight_ref[index, 128 + 64 * part : 192 + 64 * part] = low

            key = fields_ref[index, tile, 0:1, :].astype(jnp.int32)
            inside = jnp.broadcast_to(jnp.where(key == box + 1, 1.0, 0.0), (256, TILE)).astype(BF16)
            weights = weight_ref[index] * inside
            both = lax.dot_general(weights, wave_ref[index, 0], NT, preferred_element_type=F32)
            rest = lax.dot_general(
                weights[0:128], wave_ref[index, 1], NT, preferred_element_type=F32
            )
            leaf_ref[index] += both[0:128] + (both[128:256] + rest)

    low_bit = info_ref[4, 0]
    high_bit = info_ref[4, 1]
    matrix = jnp.concatenate([one_ref[low_bit, low_bit], one_ref[1 - low_bit, low_bit]], axis=1)

    def first_level(index):
        parts = []
        for child in (index, index + 1):
            real_cos = leaf_ref[child, 0:64, 0:256]
            real_sin = leaf_ref[child, 0:64, 256:512]
            imag_cos = leaf_ref[child, 64:128, 0:256]
            imag_sin = leaf_ref[child, 64:128, 256:512]
            parts.append(jnp.concatenate([real_cos - imag_sin, real_cos + imag_sin], axis=1))
            parts.append(jnp.concatenate([real_sin + imag_cos, imag_cos - real_sin], axis=1))
        return product(matrix, jnp.concatenate(parts, axis=0))

    partner_ref[0] = first_level(2)
    own = rotate(first_level(0), phase_ref[0])
    own_ref[0] = product(two_ref[high_bit, high_bit], own)


def rotate(coef, angle):
    cosine, sine = cos_sin(angle * 0.5, 1, 1.5708, 5, 6)
    real_part = coef[:64]
    imag_part = coef[64:]
    return jnp.concatenate(
        [cosine * real_part - sine * imag_part, sine * real_part + cosine * imag_part], axis=0
    )


def image_kernel(info_ref, partner_ref, own_ref, one_ref, two_ref, matrix_ref, pixel_ref, *rest):
    out_ref = rest[-1]
    high_bit = info_ref[4, 1]
    first = rotate(partner_ref[0], one_ref[0])
    second = own_ref[0] + product(matrix_ref[1 - high_bit, high_bit], first)
    out_ref[0] = product(pixel_ref[...], rotate(second, two_ref[0]))


def whole(shape):
    return pl.BlockSpec(shape, lambda *_: (0,) * len(shape))


def params():
    return pltpu.CompilerParams(vmem_limit_bytes=VMEM_LIMIT)


def from_quad(value, mask):
    pairs = [(source, source ^ mask) for source in range(lax.axis_size("quad"))]
    return lax.ppermute(value, "quad", pairs)


def image_part(info, partner, own, partner_phase, phase_two, level_two, pixel, done, begin):
    boxes, _, targets = own.shape
    count = partner_phase.shape[0]

    def moved(height):
        return pl.BlockSpec((1, height, targets), lambda b, *_: (b + begin, 0, 0))

    in_specs = [
        moved(128),
        moved(128),
        pl.BlockSpec((1, 64, targets), lambda b, *_: (b, 0, 0)),
        moved(64),
        whole(level_two.shape),
        whole(pixel.shape),
    ]
    operands = [partner, own, partner_phase, phase_two, level_two, pixel]
    aliases = {}
    if done is not None:
        in_specs.append(pl.BlockSpec(memory_space=pl.ANY))
        operands.append(done)
        aliases = {len(operands): 0}
    return pl.pallas_call(
        image_kernel,
        grid_spec=pltpu.PrefetchScalarGridSpec(
            num_scalar_prefetch=1, grid=(count,), in_specs=in_specs, out_specs=moved(128)
        ),
        out_shape=jax.ShapeDtypeStruct((boxes, 128, targets), F32),
        input_output_aliases=aliases,
        compiler_params=params(),
        name="image_part",
    )(info, *operands)


def body(sample_box, sample_coords, sample_values, level_one, level_two, phase_one, phase_two):
    senders = lax.axis_size("box")
    boxes = phase_one.shape[1]
    targets = phase_one.shape[3]
    tiles = senders * SLOTS // 128
    half = boxes // 2
    phase_one = phase_one[0]
    phase_two = phase_two[0]

    early_phase = from_quad(phase_one[:half], 2)

    packed = pl.pallas_call(
        pack_kernel,
        out_shape=jax.ShapeDtypeStruct((senders * 4, 128), F32),
        compiler_params=params(),
        name="pack",
    )(sample_box.reshape(1, -1), sample_coords, sample_values)
    arrived = lax.all_to_all(
        packed.reshape(senders, 4, 128), "box", split_axis=0, concat_axis=0, tiled=True
    )
    ordered = pl.pallas_call(
        sort_kernel,
        out_shape=jax.ShapeDtypeStruct((tiles + 3, 8, 128), F32),
        scratch_shapes=[pltpu.VMEM((8, tiles * 128), F32)],
        compiler_params=params(),
        name="sort",
    )(arrived.reshape(senders * 4, 128))
    groups = [ordered] + [from_quad(ordered, mask) for mask in (1, 2, 3)]
    late_source, _ = lax.optimization_barrier((phase_one[half:], ordered))
    late_phase = from_quad(late_source, 2)

    quad_index = lax.axis_index("quad")
    bits = jnp.zeros((24,), jnp.int32).at[0].set(quad_index % 2).at[1].set(quad_index // 2)
    starts = [group[tiles:, :, 0].reshape(24).astype(jnp.int32) for group in groups]
    info = jnp.stack(starts + [bits], axis=0)

    angles = 2.0 * np.pi * np.arange(256) / targets
    circle = np.stack([np.cos(angles), np.sin(angles)]) * (WAVENUMBER / 8.0)
    circle = jnp.asarray(np.repeat(circle[:, :, None], 128, axis=2), F32)

    def moved(height):
        return pl.BlockSpec((1, height, targets), lambda b, *_: (b, 0, 0))

    partner, own = pl.pallas_call(
        leaf_kernel,
        grid_spec=pltpu.PrefetchScalarGridSpec(
            num_scalar_prefetch=1,
            grid=(boxes,),
            in_specs=[whole(ordered.shape)] * 4
            + [whole(circle.shape), whole(level_one.shape), whole(level_two.shape), moved(64)],
            out_specs=[moved(128), moved(128)],
            scratch_shapes=[
                pltpu.VMEM((4, tiles // 2, 8, TILE), F32),
                pltpu.VMEM((4, 2, 512, TILE), BF16),
                pltpu.VMEM((4, 256, TILE), BF16),
                pltpu.VMEM((4, 128, 512), F32),
                pltpu.SMEM((4,), jnp.int32),
            ],
        ),
        out_shape=[jax.ShapeDtypeStruct((boxes, 128, targets), F32)] * 2,
        compiler_params=params(),
        name="leaf",
    )(info, *groups, circle, level_one, level_two, phase_one)

    pixel = jnp.asarray(pixel_matrix())
    image = image_part(info, partner, own, early_phase, phase_two, level_two, pixel, None, 0)
    image = image_part(info, partner, own, late_phase, phase_two, level_two, pixel, image, half)
    return image[None]


def solution(mesh):
    placed = (
        P(("quad", "box")),
        P(None, ("quad", "box")),
        P(None, ("quad", "box")),
        P(),
        P(),
        P("quad", "box", None, None),
        P("quad", "box", None, None),
    )
    return jax.shard_map(
        body, mesh=mesh, in_specs=placed, out_specs=P("quad", "box", None, None), check_vma=False
    )
```

```python
import functools

import jax
import jax.numpy as jnp
import numpy as np
from jax import lax
from jax.experimental import pallas as pl
from jax.experimental.pallas import tpu as pltpu
from jax.sharding import PartitionSpec as P

WAVENUMBER = 6.0
SLOTS = 64
TILE = 256
EARLY = 4

F32 = jnp.float32
BF16 = jnp.bfloat16
NN = (((1,), (0,)), ((), ()))
NT = (((1,), (1,)), ((), ()))


def node_table():
    nodes = np.cos(np.pi * (2.0 * np.arange(8) + 1.0) / 16.0)
    scales = []
    for center in range(8):
        product = 1.0
        for other_node in range(8):
            if other_node != center:
                product = product * (nodes[center] - nodes[other_node])
        scales.append(1.0 / product)
    return ([float(v) for v in nodes], scales)


def lagrange_rows(points):
    nodes, scales = node_table()
    row = lax.broadcasted_iota(jnp.int32, (8, points.shape[1]), 0)
    factor = None
    for node in range(8):
        term = jnp.where(row == node, scales[node], points - nodes[node])
        factor = term if factor is None else factor * term
    return factor


def pixel_matrix():
    nodes, scales = node_table()
    pixels = -1.0 + (2.0 * np.arange(8) + 1.0) / 8.0
    weights = np.zeros((8, 8))
    for center in range(8):
        value = np.full(8, scales[center])
        for other_node in range(8):
            if other_node != center:
                value = value * (pixels - nodes[other_node])
        weights[center] = value
    one_part = np.einsum("ki,mj->ijkm", weights, weights).reshape(64, 64)
    return np.kron(np.eye(2), one_part).astype(np.float32)


def series(function, limit, terms):
    grid = 0.5 * limit * limit * (1.0 - np.cos(np.pi * (np.arange(400) + 0.5) / 400))
    values = function(np.sqrt(grid))
    fit = np.polynomial.chebyshev.Chebyshev.fit(grid, values, terms - 1, domain=[0, limit * limit])
    return [float(v) for v in fit.convert(kind=np.polynomial.Polynomial).coef]


def horner(coefs, square):
    total = coefs[-1]
    for coef in coefs[-2::-1]:
        total = total * square + coef
    return total


def cos_sin(half_turns):
    square = half_turns * half_turns
    sine = horner(SINE, square) * half_turns
    cosine = horner(COSINE, square)
    twice = sine + sine
    return 1.0 - twice * sine, twice * cosine


SINE = series(lambda x: np.pi * np.sinc(x), 0.5001, 5)
COSINE = series(lambda x: np.cos(np.pi * x), 0.5001, 6)
ROUNDER = np.float32(1.5 * 2**23)


def cos_sin_turns(turns):
    return cos_sin(turns - ((turns + ROUNDER) - ROUNDER))


def split_two(value):
    high = value.astype(BF16)
    return high, (value - high.astype(F32)).astype(BF16)


def split_three(value):
    high = value.astype(BF16)
    rest = value - high.astype(F32)
    middle = rest.astype(BF16)
    low = (rest - middle.astype(F32)).astype(BF16)
    return high, middle, low


def dot(left, right, dims=NN):
    return lax.dot_general(left, right, dims, preferred_element_type=F32)


def deep_product(matrix, right):
    high, low = split_two(matrix)
    right_high, right_low = split_two(right)
    both = dot(jnp.concatenate([high, low], axis=0), right_high, NT)
    return both[:128] + (both[128:] + dot(high, right_low, NT))


def stacked_halves(matrix):
    high, low = split_two(matrix)
    top = jnp.concatenate([high, high], axis=1)
    bottom = jnp.concatenate([low, jnp.zeros_like(low)], axis=1)
    return jnp.concatenate([top, bottom], axis=0)


def product_128(stacked, right):
    both = dot(stacked, jnp.concatenate(split_two(right), axis=0))
    return both[:128] + both[128:]


def strict_upper(size):
    rows = lax.broadcasted_iota(jnp.int32, (size, size), 0)
    columns = lax.broadcasted_iota(jnp.int32, (size, size), 1)
    return jnp.where(rows < columns, 1.0, 0.0).astype(BF16)


def copy_kernel(in_ref, out_ref):
    out_ref[...] = in_ref[...]


def pack_kernel(box_ref, coords_ref, values_ref, out_ref):
    pairs = out_ref.shape[0]
    rows = box_ref.shape[1]
    tri = strict_upper(256)
    owner_ids = lax.broadcasted_iota(jnp.int32, (2 * pairs, 256), 0)
    row_pair = lax.broadcasted_iota(jnp.int32, (pairs * 4, 256), 0) >> 2
    lane_ids = lax.broadcasted_iota(jnp.int32, (4 * SLOTS, 256), 0)
    carry = jnp.zeros((2 * pairs, 1), F32)
    total = jnp.zeros((pairs * 4 * 3, 4 * SLOTS), F32)
    for start in range(0, rows, 256):
        box = box_ref[:, start : start + 256]
        owner = box >> 4
        mark = jnp.where(owner_ids == owner, 1.0, 0.0)
        ahead = dot(mark.astype(BF16), tri) + carry
        carry = carry + jnp.sum(mark, axis=1, keepdims=True)
        slot = jnp.sum(mark * ahead, axis=0, keepdims=True).astype(jnp.int32)
        slot = slot + (owner & 1) * (2 * SLOTS)
        key = ((box & 15) + 1).astype(F32)
        coords = coords_ref[:, start : start + 256]
        values = values_ref[:, start : start + 256]
        empty = jnp.zeros_like(key)
        low_fields = jnp.concatenate([key, coords[0:3]], axis=0)
        high_fields = jnp.concatenate([coords[3:4], values, empty], axis=0)
        hit = row_pair == (owner >> 1)
        for fields, shift in ((low_fields, 0), (high_fields, SLOTS)):
            place = jnp.where(lane_ids == slot + shift, 1.0, 0.0).astype(BF16)
            left = spread_parts(jnp.concatenate([fields, fields], axis=0), hit)
            total = total + dot(left, place, NT)
    total = sum_parts(total).reshape(pairs, 4, 4 * SLOTS)
    out_ref[:, 0:4, :] = total[:, :, : 2 * SLOTS]
    out_ref[:, 4:8, :] = total[:, :, 2 * SLOTS :]


def spread_parts(fields, hit):
    rows = hit.shape[0]
    out = []
    for part in split_three(fields):
        wide = part.astype(F32)
        wide = jnp.broadcast_to(wide[None], (rows // 8, 8, 256)).reshape(rows, 256)
        out.append(jnp.where(hit, wide, 0.0).astype(BF16))
    return jnp.concatenate(out, axis=0)


def sum_parts(total):
    rows = total.shape[0] // 3
    return (total[:rows] + total[rows : 2 * rows]) + total[2 * rows :]


def sort_kernel(in_ref, out_ref, fields_ref):
    pairs = in_ref.shape[0]
    tiles = out_ref.shape[0] - 1
    lane = lax.broadcasted_iota(jnp.int32, (4, 128), 1)
    for pair in range(pairs):
        first = in_ref[pair, 0:4, :]
        second = in_ref[pair, 4:8, :]
        low = jnp.where(lane < SLOTS, first, pltpu.roll(second, SLOTS, 1))
        high = jnp.where(lane < SLOTS, pltpu.roll(first, SLOTS, 1), second)
        fields_ref[:, 128 * pair : 128 * (pair + 1)] = jnp.concatenate([low, high], axis=0)
    width = tiles * TILE
    tri = strict_upper(256)
    ids = lax.broadcasted_iota(jnp.int32, (16, 256), 0) + 1
    below = jnp.zeros((16, 256), F32)
    every = jnp.zeros((1, 256), F32)
    for start in range(0, width, 256):
        key = fields_ref[0:1, start : start + 256].astype(jnp.int32)
        below = below + jnp.where((key >= 1) & (key < ids), 1.0, 0.0)
        every = every + jnp.where(key >= 1, 1.0, 0.0)
    base = jnp.sum(below, axis=1, keepdims=True)
    count = jnp.sum(every, axis=1, keepdims=True)
    tile_ids = lax.broadcasted_iota(jnp.int32, (tiles * 8, 256), 0) >> 3
    lane_ids = lax.broadcasted_iota(jnp.int32, (TILE, 256), 0)
    carry = base
    total = jnp.zeros((tiles * 8 * 3, TILE), F32)
    for start in range(0, width, 256):
        fields = fields_ref[:, start : start + 256]
        key = fields[0:1].astype(jnp.int32)
        mark = jnp.where(key == ids, 1.0, 0.0)
        ahead = dot(mark.astype(BF16), tri) + carry
        carry = carry + jnp.sum(mark, axis=1, keepdims=True)
        spot = jnp.sum(mark * ahead, axis=0, keepdims=True).astype(jnp.int32)
        spot = jnp.where(key >= 1, spot, -1)
        hit = tile_ids == (spot >> 8)
        place = jnp.where(lane_ids == (spot & 255), 1.0, 0.0).astype(BF16)
        total = total + dot(spread_parts(fields, hit), place, NT)
    out_ref[0:tiles] = sum_parts(total).reshape(tiles, 8, TILE)
    begin = lax.broadcasted_iota(jnp.int32, (16, TILE), 1).astype(F32) * TILE
    end = jnp.minimum(begin + (TILE - 1), jnp.broadcast_to(count, (16, TILE)) - 1.0)
    first_box = jnp.sum(jnp.where(base <= begin, 1.0, 0.0), axis=0, keepdims=True) - 1.0
    last_box = jnp.sum(jnp.where(base <= end, 1.0, 0.0), axis=0, keepdims=True) - 1.0
    full = jnp.where(begin[0:1] < jnp.broadcast_to(count, (1, TILE)), 1.0, 0.0)
    full = jnp.sum(full, axis=1, keepdims=True)
    row = lax.broadcasted_iota(jnp.int32, (8, TILE), 0)
    out_ref[tiles] = jnp.where(row == 0, first_box, jnp.where(row == 1, last_box, full))


LEAF_STEP = 2
IMAGE_STEP = 4


def leaf_kernel(bits_ref, *refs):
    fields_refs = refs[:4]
    circle_ref, one_ref, two_ref, phase_ref, partner_ref, own_ref, weight_ref, leaf_ref = refs[4:12]
    waves = refs[12:16]
    facts_ref, sems = refs[16:]
    tiles = fields_refs[0].shape[0] - 1
    step = pl.program_id(0)

    def fact(index, row, tile):
        return facts_ref[index, row, tile].astype(jnp.int32)

    def accumulate(index, tile, box, weights, high, low):
        key = fields_refs[index][tile, 0:1, :].astype(jnp.int32)
        kept = []
        for b in (box, box + 1):
            inside = jnp.broadcast_to(jnp.where(key == b + 1, 1.0, 0.0), (128, TILE)).astype(BF16)
            kept.append([half * inside for half in weights])
        right_high = jnp.concatenate([kept[0][0], kept[1][0]], axis=0)
        right_low = jnp.concatenate([kept[0][1], kept[1][1]], axis=0)
        total = dot(
            jnp.concatenate([high, low, high], axis=1),
            jnp.concatenate([right_high, right_high, right_low], axis=1),
            NT,
        )
        leaf_ref[index, box] += total[:, 0:128]
        leaf_ref[index, box + 1] += total[:, 128:256]

    def make_weights(fields):
        first_axis = lagrange_rows(fields[1:2])
        second_axis = lagrange_rows(fields[2:3])
        rows = []
        for part in range(2):
            scaled = second_axis * fields[5 + part : 6 + part]
            rows += [first_axis[k : k + 1] * scaled for k in range(8)]
        return split_two(jnp.concatenate(rows, axis=0))

    def make_waves(fields):
        cosines = []
        sines = []
        for row in range(0, 256, 32):
            across = circle_ref[0, row : row + 32]
            along = circle_ref[1, row : row + 32]
            turns = (
                jnp.concatenate([across, across], axis=1) * fields[3:4]
                + jnp.concatenate([along, along], axis=1) * fields[4:5]
            )
            cosine, sine = cos_sin_turns(turns)
            cosines.append(split_two(cosine))
            sines.append(split_two(sine))
        return [jnp.concatenate([v[k] for v in cosines + sines], axis=0) for k in range(2)]

    @pl.when(step == 0)
    def _():
        copies = [
            pltpu.make_async_copy(fields_refs[index].at[tiles], facts_ref.at[index], sems.at[index])
            for index in range(4)
        ]
        for copy in copies:
            copy.start()

        @pl.loop(0, 4)
        def _(index):
            @pl.loop(0, leaf_ref.shape[1])
            def _(box):
                leaf_ref[index, box] = jnp.zeros_like(leaf_ref[index, box])

        for copy in copies:
            copy.wait()
        steps = fact(0, 2, 0)
        for index in range(1, 4):
            steps = jnp.maximum(steps, fact(index, 2, 0))

        @pl.loop(0, steps)
        def _(tile):
            for index in range(4):
                fields = fields_refs[index][tile]
                high, low = make_waves(fields)
                weights = make_weights(fields)
                waves[index][0] = high
                waves[index][1] = low
                weight_ref[index, 0] = weights[0]
                weight_ref[index, 1] = weights[1]
                accumulate(index, tile, fact(index, 0, tile), weights, high, low)
            for index in range(4):
                first_box = fact(index, 0, tile)
                last_box = fact(index, 1, tile)

                @pl.loop(1, (last_box - first_box) // 2 + 1)
                def _(group):
                    accumulate(
                        index,
                        tile,
                        first_box + 2 * group,
                        (weight_ref[index, 0], weight_ref[index, 1]),
                        waves[index][0],
                        waves[index][1],
                    )

    @pl.when(step > 0)
    def _():
        low_bit = bits_ref[0]
        high_bit = bits_ref[1]
        matrix = jnp.concatenate([one_ref[low_bit, low_bit], one_ref[1 - low_bit, low_bit]], axis=1)
        second = stacked_halves(two_ref[high_bit, high_bit])
        sign = jnp.where(lax.broadcasted_iota(jnp.int32, (256, 128), 1) < 64, -1.0, 1.0)

        def first_level(index, box):
            parts = []
            for child in (index, index + 1):
                even = leaf_ref[child, box, 0:256]
                odd = pltpu.roll(leaf_ref[child, box, 256:512], 64, 1) * sign
                parts.append(jnp.concatenate([even + odd, even - odd], axis=0))
            return deep_product(matrix, jnp.concatenate(parts, axis=1))

        owns = {}
        for k in range(LEAF_STEP + 1):
            box = (step - 1) * LEAF_STEP + k
            if k < LEAF_STEP:
                owns[k] = first_level(0, box)
                partner_ref[k] = first_level(2, box)
            if k > 0:
                own_ref[k - 1] = product_128(second, rotate(owns[k - 1], phase_ref[k - 1]))


def rotate(coef, angle):
    cosine, sine = cos_sin(angle * np.float32(0.5 / np.pi))
    real_part = coef[:64]
    imag_part = coef[64:]
    return jnp.concatenate(
        [cosine * real_part - sine * imag_part, sine * real_part + cosine * imag_part], axis=0
    )


def image_kernel(
    bits_ref, partner_ref, own_ref, early_ref, late_ref, two_ref, matrix_ref, pixel_ref, out_ref
):
    high_bit = bits_ref[1]
    matrix = stacked_halves(matrix_ref[1 - high_bit, high_bit])
    pixel = stacked_halves(pixel_ref[...])
    early = early_ref.shape[0]
    seconds = {}
    images = {}
    for k in range(IMAGE_STEP + 2):
        if k < IMAGE_STEP:
            box = pl.program_id(0) * IMAGE_STEP + k
            phase = jnp.where(
                box < early,
                early_ref[jnp.minimum(box, early - 1)],
                late_ref[jnp.maximum(box - early, 0)],
            )
            first = rotate(partner_ref[k], phase)
            seconds[k] = own_ref[k] + product_128(matrix, first)
        if 1 <= k <= IMAGE_STEP:
            images[k - 1] = product_128(pixel, rotate(seconds[k - 1], two_ref[k - 1]))
        if k >= 2:
            out_ref[k - 2] = images[k - 2]


def whole(shape):
    return pl.BlockSpec(shape, lambda *_: (0,) * len(shape))


def params(mebibytes=24):
    return pltpu.CompilerParams(vmem_limit_bytes=mebibytes * 1024 * 1024)


def from_quad(value, mask):
    pairs = [(source, source ^ mask) for source in range(lax.axis_size("quad"))]
    return lax.ppermute(value, "quad", pairs)


def part_of(array, begin, count):
    block = (4,) + array.shape[1:]
    return pl.pallas_call(
        copy_kernel,
        grid=(count // 4,),
        in_specs=[pl.BlockSpec(block, lambda b: (b + begin // 4, 0, 0))],
        out_specs=pl.BlockSpec(block, lambda b: (b, 0, 0)),
        out_shape=jax.ShapeDtypeStruct((count,) + array.shape[1:], F32),
        compiler_params=params(),
        name="part_of",
    )(array)


def body(sample_box, sample_coords, sample_values, level_one, level_two, phase_one, phase_two):
    senders = lax.axis_size("box")
    boxes = phase_one.shape[1]
    targets = phase_one.shape[3]
    tiles = senders * SLOTS // TILE
    early = EARLY
    phase_one = phase_one[0]
    phase_two = phase_two[0]

    early_source = part_of(phase_one, 0, early)
    early_phase = from_quad(early_source, 2)
    sample_box, _ = lax.optimization_barrier((sample_box, early_source))

    packed = pl.pallas_call(
        pack_kernel,
        out_shape=jax.ShapeDtypeStruct((senders // 2, 8, 128), F32),
        compiler_params=params(),
        name="pack",
    )(sample_box.reshape(1, -1), sample_coords, sample_values)
    arrived = lax.all_to_all(
        packed.reshape(senders, 4, 128), "box", split_axis=0, concat_axis=0, tiled=True
    )
    arrived, early_phase = lax.optimization_barrier((arrived, early_phase))
    ordered = pl.pallas_call(
        sort_kernel,
        out_shape=jax.ShapeDtypeStruct((tiles + 1, 8, TILE), F32),
        scratch_shapes=[pltpu.VMEM((8, tiles * TILE), F32)],
        compiler_params=params(),
        name="sort",
    )(arrived.reshape(senders // 2, 8, 128))
    groups = [ordered] + [from_quad(ordered, mask) for mask in (1, 2, 3)]
    late_source = part_of(phase_one, early, boxes - early)
    late_source, *groups = lax.optimization_barrier((late_source, *groups))
    late_phase = from_quad(late_source, 2)

    quad_index = lax.axis_index("quad")
    bits = jnp.stack([quad_index % 2, quad_index // 2])

    angles = 2.0 * np.pi * np.arange(256) / targets
    circle = np.stack([np.cos(angles), np.sin(angles)]) * (WAVENUMBER / (2.0 * np.pi))
    circle = jnp.asarray(np.repeat(circle[:, :, None], 128, axis=2), F32)

    def moved(height):
        return pl.BlockSpec(
            (LEAF_STEP, height, targets), lambda b, *_: (jnp.maximum(b - 1, 0), 0, 0)
        )

    partner, own = pl.pallas_call(
        leaf_kernel,
        grid_spec=pltpu.PrefetchScalarGridSpec(
            num_scalar_prefetch=1,
            grid=(1 + boxes // LEAF_STEP,),
            in_specs=[whole(ordered.shape)] * 4
            + [whole(circle.shape), whole(level_one.shape), whole(level_two.shape), moved(64)],
            out_specs=[moved(128), moved(128)],
            scratch_shapes=[
                pltpu.VMEM((4, 2, 128, TILE), BF16),
                pltpu.VMEM((4, boxes + 1, 512, 128), F32),
            ]
            + [pltpu.VMEM((2, 512, TILE), BF16)] * 4
            + [pltpu.SMEM((4, 8, TILE), F32), pltpu.SemaphoreType.DMA((4,))],
        ),
        out_shape=[jax.ShapeDtypeStruct((boxes, 128, targets), F32)] * 2,
        compiler_params=params(40),
        name="leaf",
    )(bits, *groups, circle, level_one, level_two, phase_one)

    pixel = jnp.asarray(pixel_matrix())

    def along(height):
        return pl.BlockSpec((IMAGE_STEP, height, targets), lambda b, *_: (b, 0, 0))

    kept = pl.BlockSpec(memory_space=pltpu.VMEM)
    image = pl.pallas_call(
        image_kernel,
        grid_spec=pltpu.PrefetchScalarGridSpec(
            num_scalar_prefetch=1,
            grid=(boxes // IMAGE_STEP,),
            in_specs=[along(128), along(128), kept, kept, along(64)]
            + [whole(level_two.shape), whole(pixel.shape)],
            out_specs=along(128),
        ),
        out_shape=jax.ShapeDtypeStruct((boxes, 128, targets), F32),
        compiler_params=params(),
        name="image",
    )(bits, partner, own, early_phase, late_phase, phase_two, level_two, pixel)
    return image[None]


def solution(mesh):
    placed = (
        P(("quad", "box")),
        P(None, ("quad", "box")),
        P(None, ("quad", "box")),
        P(),
        P(),
        P("quad", "box", None, None),
        P("quad", "box", None, None),
    )
    return jax.shard_map(
        body, mesh=mesh, in_specs=placed, out_specs=P("quad", "box", None, None), check_vma=False
    )
```

```python
import functools

import jax
import jax.numpy as jnp
import numpy as np
from jax import lax
from jax.experimental import pallas as pl
from jax.experimental.pallas import tpu as pltpu
from jax.sharding import PartitionSpec as P

WAVENUMBER = 6.0
SLOTS = 64
TILE = 128
BLOCKS = 24
EARLY = 6

F32 = jnp.float32
BF16 = jnp.bfloat16
NN = (((1,), (0,)), ((), ()))
NT = (((1,), (1,)), ((), ()))


def node_table():
    nodes = np.cos(np.pi * (2.0 * np.arange(8) + 1.0) / 16.0)
    scales = []
    for center in range(8):
        product = 1.0
        for other_node in range(8):
            if other_node != center:
                product = product * (nodes[center] - nodes[other_node])
        scales.append(1.0 / product)
    return ([float(v) for v in nodes], scales)


def lagrange_rows(points):
    nodes, scales = node_table()
    row = lax.broadcasted_iota(jnp.int32, (8, points.shape[1]), 0)
    factor = None
    for node in range(8):
        term = jnp.where(row == node, scales[node], points - nodes[node])
        factor = term if factor is None else factor * term
    return factor


def pixel_matrix():
    nodes, scales = node_table()
    pixels = -1.0 + (2.0 * np.arange(8) + 1.0) / 8.0
    weights = np.zeros((8, 8))
    for center in range(8):
        value = np.full(8, scales[center])
        for other_node in range(8):
            if other_node != center:
                value = value * (pixels - nodes[other_node])
        weights[center] = value
    one_part = np.einsum("ki,mj->ijkm", weights, weights).reshape(64, 64)
    return np.kron(np.eye(2), one_part).astype(np.float32)


def series(function, limit, terms):
    grid = 0.5 * limit * limit * (1.0 - np.cos(np.pi * (np.arange(400) + 0.5) / 400))
    values = function(np.sqrt(grid))
    fit = np.polynomial.chebyshev.Chebyshev.fit(grid, values, terms - 1, domain=[0, limit * limit])
    return [float(v) for v in fit.convert(kind=np.polynomial.Polynomial).coef]


def horner(coefs, square):
    total = coefs[-1]
    for coef in coefs[-2::-1]:
        total = total * square + coef
    return total


def cos_sin(half_turns):
    square = half_turns * half_turns
    sine = horner(SINE, square) * half_turns
    cosine = horner(COSINE, square)
    twice = sine + sine
    return 1.0 - twice * sine, twice * cosine


SINE = series(lambda x: np.pi * np.sinc(x), 0.5001, 5)
COSINE = series(lambda x: np.cos(np.pi * x), 0.5001, 5)
ROUNDER = np.float32(1.5 * 2**23)


def cos_sin_turns(turns):
    return cos_sin(turns - ((turns + ROUNDER) - ROUNDER))


def split_two(value):
    high = value.astype(BF16)
    return high, (value - high.astype(F32)).astype(BF16)


def split_three(value):
    high = value.astype(BF16)
    rest = value - high.astype(F32)
    middle = rest.astype(BF16)
    low = (rest - middle.astype(F32)).astype(BF16)
    return high, middle, low


def dot(left, right, dims=NN):
    return lax.dot_general(left, right, dims, preferred_element_type=F32)


def deep_product(matrix, right):
    high, low = split_two(matrix)
    right_high, right_low = split_two(right)
    both = dot(jnp.concatenate([high, low], axis=0), right_high, NT)
    return both[:128] + (both[128:] + dot(high, right_low, NT))


def stacked_halves(matrix):
    high, low = split_two(matrix)
    top = jnp.concatenate([high, high], axis=1)
    bottom = jnp.concatenate([low, jnp.zeros_like(low)], axis=1)
    return jnp.concatenate([top, bottom], axis=0)


def product_128(stacked, right):
    both = dot(stacked, jnp.concatenate(split_two(right), axis=0))
    return both[:128] + both[128:]


def strict_upper(size):
    rows = lax.broadcasted_iota(jnp.int32, (size, size), 0)
    columns = lax.broadcasted_iota(jnp.int32, (size, size), 1)
    return jnp.where(rows < columns, 1.0, 0.0).astype(BF16)


def pack_kernel(box_ref, coords_ref, values_ref, phase_ref, out_ref, early_ref, late_ref):
    early_ref[...] = phase_ref[: early_ref.shape[0]]
    late_ref[...] = phase_ref[early_ref.shape[0] :]
    pairs = out_ref.shape[0]
    rows = box_ref.shape[1]
    tri = strict_upper(256)
    owner_ids = lax.broadcasted_iota(jnp.int32, (2 * pairs, 256), 0)
    row_pair = lax.broadcasted_iota(jnp.int32, (pairs * 4, 256), 0) >> 2
    lane_ids = lax.broadcasted_iota(jnp.int32, (4 * SLOTS, 256), 0)
    carry = jnp.zeros((2 * pairs, 1), F32)
    total = jnp.zeros((pairs * 4 * 3, 4 * SLOTS), F32)
    for start in range(0, rows, 256):
        box = box_ref[:, start : start + 256]
        owner = box >> 4
        mark = jnp.where(owner_ids == owner, 1.0, 0.0)
        ahead = dot(mark.astype(BF16), tri) + carry
        carry = carry + jnp.sum(mark, axis=1, keepdims=True)
        slot = jnp.sum(mark * ahead, axis=0, keepdims=True).astype(jnp.int32)
        slot = slot + (owner & 1) * (2 * SLOTS)
        key = ((box & 15) + 1).astype(F32)
        coords = coords_ref[:, start : start + 256]
        values = values_ref[:, start : start + 256]
        empty = jnp.zeros_like(key)
        low_fields = jnp.concatenate([key, coords[0:3]], axis=0)
        high_fields = jnp.concatenate([coords[3:4], values, empty], axis=0)
        hit = row_pair == (owner >> 1)
        for fields, shift in ((low_fields, 0), (high_fields, SLOTS)):
            place = jnp.where(lane_ids == slot + shift, 1.0, 0.0).astype(BF16)
            left = spread_parts(jnp.concatenate([fields, fields], axis=0), hit)
            total = total + dot(left, place, NT)
    total = sum_parts(total).reshape(pairs, 4, 4 * SLOTS)
    out_ref[:, 0:4, :] = total[:, :, : 2 * SLOTS]
    out_ref[:, 4:8, :] = total[:, :, 2 * SLOTS :]


def spread_parts(fields, hit):
    rows = hit.shape[0]
    out = []
    for part in split_three(fields):
        wide = part.astype(F32)
        wide = jnp.broadcast_to(wide[None], (rows // 8, 8, 256)).reshape(rows, 256)
        out.append(jnp.where(hit, wide, 0.0).astype(BF16))
    return jnp.concatenate(out, axis=0)


def sum_parts(total):
    rows = total.shape[0] // 3
    return (total[:rows] + total[rows : 2 * rows]) + total[2 * rows :]


def sort_kernel(in_ref, out_ref, fields_ref):
    pairs = in_ref.shape[0]
    blocks = out_ref.shape[0] - 1
    lane = lax.broadcasted_iota(jnp.int32, (4, 128), 1)
    for pair in range(pairs):
        first = in_ref[pair, 0:4, :]
        second = in_ref[pair, 4:8, :]
        low = jnp.where(lane < SLOTS, first, pltpu.roll(second, SLOTS, 1))
        high = jnp.where(lane < SLOTS, pltpu.roll(first, SLOTS, 1), second)
        fields_ref[:, 128 * pair : 128 * (pair + 1)] = jnp.concatenate([low, high], axis=0)
    width = pairs * 128
    tri = strict_upper(256)
    ids = lax.broadcasted_iota(jnp.int32, (16, 256), 0) + 1
    count = jnp.zeros((16, 256), F32)
    for start in range(0, width, 256):
        key = fields_ref[0:1, start : start + 256].astype(jnp.int32)
        count = count + jnp.where(key == ids, 1.0, 0.0)
    count = jnp.sum(count, axis=1, keepdims=True).astype(jnp.int32)
    used = ((count + (TILE - 1)) >> 7).astype(F32)
    rows = lax.broadcasted_iota(jnp.int32, (16, 16), 0)
    columns = lax.broadcasted_iota(jnp.int32, (16, 16), 1)
    before = jnp.where(columns < rows, 1.0, 0.0).astype(BF16)
    first_tile = dot(before, jnp.broadcast_to(used, (16, 128)).astype(BF16))[:, 0:1]
    tile_ids = lax.broadcasted_iota(jnp.int32, (blocks * 8, 256), 0) >> 3
    lane_ids = lax.broadcasted_iota(jnp.int32, (256, 256), 0)
    carry = first_tile * TILE
    total = jnp.zeros((blocks * 8 * 3, 256), F32)
    for start in range(0, width, 256):
        fields = fields_ref[:, start : start + 256]
        key = fields[0:1].astype(jnp.int32)
        mark = jnp.where(key == ids, 1.0, 0.0)
        ahead = dot(mark.astype(BF16), tri) + carry
        carry = carry + jnp.sum(mark, axis=1, keepdims=True)
        spot = jnp.sum(mark * ahead, axis=0, keepdims=True).astype(jnp.int32)
        spot = jnp.where(key >= 1, spot, -1)
        hit = tile_ids == (spot >> 8)
        place = jnp.where(lane_ids == (spot & 255), 1.0, 0.0).astype(BF16)
        total = total + dot(spread_parts(fields, hit), place, NT)
    out_ref[0:blocks] = sum_parts(total).reshape(blocks, 8, 256)
    lane = lax.broadcasted_iota(jnp.int32, (16, 256), 1).astype(F32)
    box = jnp.sum(jnp.where(first_tile + used <= lane, 1.0, 0.0), axis=0, keepdims=True)
    in_use = (jnp.sum(used, axis=0, keepdims=True).astype(jnp.int32) + 1) >> 1
    row = lax.broadcasted_iota(jnp.int32, (8, 256), 0)
    out_ref[blocks] = jnp.where(row == 0, box, in_use.astype(F32))


LEAF_STEP = 4
IMAGE_STEP = 4


def add_samples(fields_refs, leaf_ref, circle_ref, facts_ref, sems):
    blocks = fields_refs[0].shape[0] - 1
    quads = range(len(fields_refs))

    def fact(index, row, lane):
        return facts_ref[index, row, lane].astype(jnp.int32)

    def make_weights(fields):
        first_axis = lagrange_rows(fields[1:2])
        second_axis = lagrange_rows(fields[2:3])
        rows = []
        for part in range(2):
            scaled = second_axis * fields[5 + part : 6 + part]
            rows += [first_axis[k : k + 1] * scaled for k in range(8)]
        return split_two(jnp.concatenate(rows, axis=0))

    def make_waves(fields):
        cosines = []
        sines = []
        for row in range(0, 256, 32):
            across = circle_ref[0, row : row + 32]
            along = circle_ref[1, row : row + 32]
            turns = (
                jnp.concatenate([across, across], axis=1) * fields[3:4]
                + jnp.concatenate([along, along], axis=1) * fields[4:5]
            )
            cosine, sine = cos_sin_turns(turns)
            cosines.append(split_two(cosine))
            sines.append(split_two(sine))
        return [jnp.concatenate([v[k] for v in cosines + sines], axis=0) for k in range(2)]

    def accumulate(index, box, waves, weights):
        high, low = weights
        right = jnp.concatenate(
            [
                jnp.concatenate([high, high], axis=1),
                jnp.concatenate([low, jnp.zeros_like(low)], axis=1),
            ],
            axis=0,
        )
        total = dot(jnp.concatenate(waves, axis=1), right, NT)
        leaf_ref[index, box] += total[:, 0:128] + total[:, 128:256]

    copies = [
        pltpu.make_async_copy(fields_refs[index].at[blocks], facts_ref.at[index], sems.at[index])
        for index in quads
    ]
    for copy in copies:
        copy.start()
    target = lax.broadcasted_iota(jnp.int32, (256, 128), 0).astype(F32)
    for k, value in enumerate(cos_sin_turns(target * (1.0 / 512.0))):
        circle_ref[k] = value * np.float32(WAVENUMBER / (2.0 * np.pi))

    @pl.loop(0, len(fields_refs))
    def _(index):
        @pl.loop(0, leaf_ref.shape[1])
        def _(box):
            leaf_ref[index, box] = jnp.zeros_like(leaf_ref[index, box])

    for copy in copies:
        copy.wait()
    steps = fact(0, 1, 0)
    for index in quads[1:]:
        steps = jnp.maximum(steps, fact(index, 1, 0))
    stride = 2 if len(quads) == 1 else 1

    @pl.loop(0, (steps + (stride - 1)) // stride)
    def _(step):
        for index, ahead in [(index, ahead) for index in quads for ahead in range(stride)]:
            block = step * stride + ahead
            fields = fields_refs[index][block]
            waves = make_waves(fields)
            weights = make_weights(fields)
            for k in range(2):
                lanes = slice(TILE * k, TILE * (k + 1))
                accumulate(
                    index,
                    fact(index, 0, 2 * block + k),
                    [half[:, lanes] for half in waves],
                    [half[:, lanes] for half in weights],
                )


def leaf_scratch(count):
    return [
        pltpu.VMEM((2, 256, 128), F32),
        pltpu.SMEM((count, 8, 2 * TILE), F32),
        pltpu.SemaphoreType.DMA((count,)),
    ]


def own_leaf_kernel(fields_ref, leaf_ref, circle_ref, facts_ref, sems):
    add_samples([fields_ref], leaf_ref, circle_ref, facts_ref, sems)


def leaf_kernel(bits_ref, *refs):
    fields_refs = refs[:3]
    own_leaf_ref, one_ref, two_ref, turn_ref = refs[3:7]
    partner_ref, own_ref, leaf_ref, circle_ref, facts_ref, sems = refs[7:]
    add_samples(fields_refs, leaf_ref, circle_ref, facts_ref, sems)
    leaves = [own_leaf_ref.at[0], leaf_ref.at[0], leaf_ref.at[1], leaf_ref.at[2]]
    low_bit = bits_ref[0]
    high_bit = bits_ref[1]
    matrix = jnp.concatenate([one_ref[low_bit, low_bit], one_ref[1 - low_bit, low_bit]], axis=1)
    second = stacked_halves(two_ref[high_bit, high_bit])
    sign = jnp.where(lax.broadcasted_iota(jnp.int32, (256, 128), 1) < 64, -1.0, 1.0)

    def first_level(index, box):
        parts = []
        for child in (index, index + 1):
            even = leaves[child][box, 0:256]
            odd = pltpu.roll(leaves[child][box, 256:512], 64, 1) * sign
            parts.append(jnp.concatenate([even + odd, even - odd], axis=0))
        return deep_product(matrix, jnp.concatenate(parts, axis=1))

    @pl.loop(0, turn_ref.shape[1], step=LEAF_STEP)
    def _(begin):
        owns = {}
        for k in range(LEAF_STEP + 1):
            if k < LEAF_STEP:
                owns[k] = first_level(0, begin + k)
                partner_ref[begin + k] = first_level(2, begin + k)
            if k > 0:
                turned = rotate_by(owns[k - 1], *[turn_ref[h, begin + k - 1] for h in range(2)])
                own_ref[begin + k - 1] = product_128(second, turned)


def turn_kernel(one_ref, two_ref, one_out, two_out):
    for angle_ref, out in ((one_ref, one_out), (two_ref, two_out)):
        for k in range(angle_ref.shape[0]):
            out[0, k], out[1, k] = cos_sin(angle_ref[k] * np.float32(0.5 / np.pi))


def rotate(coef, angle):
    return rotate_by(coef, *cos_sin(angle * np.float32(0.5 / np.pi)))


def rotate_by(coef, cosine, sine):
    real_part = coef[:64]
    imag_part = coef[64:]
    return jnp.concatenate(
        [cosine * real_part - sine * imag_part, sine * real_part + cosine * imag_part], axis=0
    )


def image_kernel(
    bits_ref, partner_ref, own_ref, early_ref, late_ref, two_ref, matrix_ref, pixel_ref, out_ref
):
    high_bit = bits_ref[1]
    matrix = stacked_halves(matrix_ref[1 - high_bit, high_bit])
    pixel = stacked_halves(pixel_ref[...])
    early = early_ref.shape[0]
    seconds = {}
    images = {}
    begin = pl.program_id(0) * IMAGE_STEP
    for k in range(IMAGE_STEP + 2):
        if k < IMAGE_STEP:
            box = begin + k
            phase = jnp.where(
                box < early,
                early_ref[jnp.minimum(box, early - 1)],
                late_ref[jnp.maximum(box - early, 0)],
            )
            first = rotate(partner_ref[box], phase)
            seconds[k] = own_ref[box] + product_128(matrix, first)
        if 1 <= k <= IMAGE_STEP:
            turned = rotate_by(
                seconds[k - 1], *[two_ref[h, begin + k - 1] for h in range(2)]
            )
            images[k - 1] = product_128(pixel, turned)
        if k >= 2:
            out_ref[k - 2] = images[k - 2]


KEPT = pl.BlockSpec(memory_space=pltpu.VMEM)


def whole(shape):
    return pl.BlockSpec(shape, lambda *_: (0,) * len(shape))


def params(mebibytes=24):
    return pltpu.CompilerParams(vmem_limit_bytes=mebibytes * 1024 * 1024)


def from_quad(value, mask):
    pairs = [(source, source ^ mask) for source in range(lax.axis_size("quad"))]
    return lax.ppermute(value, "quad", pairs)


def body(sample_box, sample_coords, sample_values, level_one, level_two, phase_one, phase_two):
    senders = lax.axis_size("box")
    boxes = phase_one.shape[1]
    targets = phase_one.shape[3]
    early = EARLY
    phase_one = phase_one[0]
    phase_two = phase_two[0]

    early_shape = (early,) + phase_one.shape[1:]
    late_shape = (boxes - early,) + phase_one.shape[1:]
    sample_box = sample_box.reshape(1, -1)
    packed_shape = (senders // 2, 8, 128)
    operands = (sample_box, sample_coords, sample_values, phase_one)
    results = (packed_shape, early_shape, late_shape)
    packed, early_source, late_source = pl.pallas_call(
        pack_kernel,
        grid=(1,),
        in_specs=[whole(v.shape) for v in operands],
        out_specs=[whole(v) for v in results],
        out_shape=[jax.ShapeDtypeStruct(v, F32) for v in results],
        compiler_params=params(60),
        name="pack",
    )(*operands)
    early_phase = from_quad(early_source, 2)
    arrived = lax.all_to_all(
        packed.reshape(senders, 4, 128), "box", split_axis=0, concat_axis=0, tiled=True
    )
    arrived, early_phase = lax.optimization_barrier((arrived, early_phase))
    ordered = pl.pallas_call(
        sort_kernel,
        out_shape=jax.ShapeDtypeStruct((BLOCKS + 1, 8, 2 * TILE), F32),
        scratch_shapes=[pltpu.VMEM((8, senders * SLOTS), F32)],
        compiler_params=params(),
        name="sort",
    )(arrived.reshape(senders // 2, 8, 128))
    others = [from_quad(ordered, mask) for mask in (1, 2, 3)]

    quad_index = lax.axis_index("quad")
    bits = jnp.stack([quad_index % 2, quad_index // 2])

    turn_in = pl.BlockSpec((2,) + phase_one.shape[1:], lambda b: (b, 0, 0))
    turn_out = pl.BlockSpec((2, 2) + phase_one.shape[1:], lambda b: (0, b, 0, 0))
    turn_one, turn_two = pl.pallas_call(
        turn_kernel,
        grid=(boxes // 2,),
        in_specs=[turn_in] * 2,
        out_specs=[turn_out] * 2,
        out_shape=[jax.ShapeDtypeStruct((2,) + phase_one.shape, F32)] * 2,
        compiler_params=params(60),
        name="turn",
    )(phase_one, phase_two)

    scalars = pl.BlockSpec(memory_space=pltpu.SMEM)
    own_leaf = pl.pallas_call(
        own_leaf_kernel,
        in_specs=[KEPT],
        out_specs=KEPT,
        out_shape=jax.ShapeDtypeStruct((1, boxes + 1, 512, 128), F32),
        scratch_shapes=leaf_scratch(1),
        compiler_params=params(24),
        cost_estimate=pl.CostEstimate(flops=9 * 10**9, bytes_accessed=8 * 10**6, transcendentals=0),
        name="own_leaf",
    )(ordered)
    late_source, *_ = lax.optimization_barrier((late_source, *others))
    late_phase = from_quad(late_source, 2)
    partner, own = pl.pallas_call(
        leaf_kernel,
        in_specs=[scalars] + [KEPT] * 7,
        out_specs=[KEPT] * 2,
        out_shape=[jax.ShapeDtypeStruct((boxes, 128, targets), F32)] * 2,
        scratch_shapes=[pltpu.VMEM((3, boxes + 1, 512, 128), F32)] + leaf_scratch(3),
        compiler_params=params(32),
        cost_estimate=pl.CostEstimate(flops=30 * 10**9, bytes_accessed=24 * 10**6, transcendentals=0),
        name="leaf",
    )(bits, *others, own_leaf, level_one, level_two, turn_one)

    pixel = jnp.asarray(pixel_matrix())

    image = pl.pallas_call(
        image_kernel,
        grid=(boxes // IMAGE_STEP,),
        in_specs=[scalars] + [KEPT] * 7,
        out_specs=pl.BlockSpec((IMAGE_STEP, 128, targets), lambda b: (b, 0, 0)),
        out_shape=jax.ShapeDtypeStruct((boxes, 128, targets), F32),
        compiler_params=params(24),
        name="image",
    )(bits, partner, own, early_phase, late_phase, turn_two, level_two, pixel)
    return image[None]


def solution(mesh):
    placed = (
        P(("quad", "box")),
        P(None, ("quad", "box")),
        P(None, ("quad", "box")),
        P(),
        P(),
        P("quad", "box", None, None),
        P("quad", "box", None, None),
    )
    return jax.shard_map(
        body, mesh=mesh, in_specs=placed, out_specs=P("quad", "box", None, None), check_vma=False
    )
```

```python
import functools

import jax
import jax.numpy as jnp
import numpy as np
from jax import lax
from jax.experimental import pallas as pl
from jax.experimental.pallas import tpu as pltpu
from jax.sharding import PartitionSpec as P

WAVENUMBER = 6.0
SLOTS = 64
TILE = 128
BLOCKS = 24
EARLY = 6

F32 = jnp.float32
BF16 = jnp.bfloat16
NN = (((1,), (0,)), ((), ()))
NT = (((1,), (1,)), ((), ()))


def node_table():
    nodes = np.cos(np.pi * (2.0 * np.arange(8) + 1.0) / 16.0)
    scales = []
    for center in range(8):
        product = 1.0
        for other_node in range(8):
            if other_node != center:
                product = product * (nodes[center] - nodes[other_node])
        scales.append(1.0 / product)
    return ([float(v) for v in nodes], scales)


def lagrange_rows(points):
    nodes, scales = node_table()
    row = lax.broadcasted_iota(jnp.int32, (8, points.shape[1]), 0)
    factor = None
    for node in range(8):
        term = jnp.where(row == node, scales[node], points - nodes[node])
        factor = term if factor is None else factor * term
    return factor


def pixel_matrix():
    nodes, scales = node_table()
    pixels = -1.0 + (2.0 * np.arange(8) + 1.0) / 8.0
    weights = np.zeros((8, 8))
    for center in range(8):
        value = np.full(8, scales[center])
        for other_node in range(8):
            if other_node != center:
                value = value * (pixels - nodes[other_node])
        weights[center] = value
    one_part = np.einsum("ki,mj->ijkm", weights, weights).reshape(64, 64)
    return np.kron(np.eye(2), one_part).astype(np.float32)


def series(function, limit, terms):
    grid = 0.5 * limit * limit * (1.0 - np.cos(np.pi * (np.arange(400) + 0.5) / 400))
    values = function(np.sqrt(grid))
    fit = np.polynomial.chebyshev.Chebyshev.fit(grid, values, terms - 1, domain=[0, limit * limit])
    return [float(v) for v in fit.convert(kind=np.polynomial.Polynomial).coef]


def horner(coefs, square):
    total = coefs[-1]
    for coef in coefs[-2::-1]:
        total = total * square + coef
    return total


def cos_sin(half_turns):
    square = half_turns * half_turns
    sine = horner(SINE, square) * half_turns
    cosine = horner(COSINE, square)
    twice = sine + sine
    return 1.0 - twice * sine, twice * cosine


SINE = series(lambda x: np.pi * np.sinc(x), 0.5001, 5)
COSINE = series(lambda x: np.cos(np.pi * x), 0.5001, 5)
ROUNDER = np.float32(1.5 * 2**23)


def cos_sin_turns(turns):
    return cos_sin(turns - ((turns + ROUNDER) - ROUNDER))


def split_two(value):
    high = value.astype(BF16)
    return high, (value - high.astype(F32)).astype(BF16)


def split_three(value):
    high = value.astype(BF16)
    rest = value - high.astype(F32)
    middle = rest.astype(BF16)
    low = (rest - middle.astype(F32)).astype(BF16)
    return high, middle, low


def dot(left, right, dims=NN):
    return lax.dot_general(left, right, dims, preferred_element_type=F32)


def deep_product(matrix, right):
    high, low = split_two(matrix)
    right_high, right_low = split_two(right)
    both = dot(jnp.concatenate([high, low], axis=0), right_high, NT)
    return both[:128] + (both[128:] + dot(high, right_low, NT))


def stacked_halves(matrix):
    high, low = split_two(matrix)
    top = jnp.concatenate([high, high], axis=1)
    bottom = jnp.concatenate([low, jnp.zeros_like(low)], axis=1)
    return jnp.concatenate([top, bottom], axis=0)


def product_128(stacked, right):
    both = dot(stacked, jnp.concatenate(split_two(right), axis=0))
    return both[:128] + both[128:]


def strict_upper(size):
    rows = lax.broadcasted_iota(jnp.int32, (size, size), 0)
    columns = lax.broadcasted_iota(jnp.int32, (size, size), 1)
    return jnp.where(rows < columns, 1.0, 0.0).astype(BF16)


def pack_kernel(box_ref, coords_ref, values_ref, phase_ref, out_ref, early_ref, late_ref):
    early_ref[...] = phase_ref[: early_ref.shape[0]]
    late_ref[...] = phase_ref[early_ref.shape[0] :]
    pairs = out_ref.shape[0]
    rows = box_ref.shape[1]
    tri = strict_upper(256)
    owner_ids = lax.broadcasted_iota(jnp.int32, (2 * pairs, 256), 0)
    row_pair = lax.broadcasted_iota(jnp.int32, (pairs * 4, 256), 0) >> 2
    lane_ids = lax.broadcasted_iota(jnp.int32, (4 * SLOTS, 256), 0)
    carry = jnp.zeros((2 * pairs, 1), F32)
    total = jnp.zeros((pairs * 4 * 3, 4 * SLOTS), F32)
    for start in range(0, rows, 256):
        box = box_ref[:, start : start + 256]
        owner = box >> 4
        mark = jnp.where(owner_ids == owner, 1.0, 0.0)
        ahead = dot(mark.astype(BF16), tri) + carry
        carry = carry + jnp.sum(mark, axis=1, keepdims=True)
        slot = jnp.sum(mark * ahead, axis=0, keepdims=True).astype(jnp.int32)
        slot = slot + (owner & 1) * (2 * SLOTS)
        key = ((box & 15) + 1).astype(F32)
        coords = coords_ref[:, start : start + 256]
        values = values_ref[:, start : start + 256]
        empty = jnp.zeros_like(key)
        low_fields = jnp.concatenate([key, coords[0:3]], axis=0)
        high_fields = jnp.concatenate([coords[3:4], values, empty], axis=0)
        hit = row_pair == (owner >> 1)
        for fields, shift in ((low_fields, 0), (high_fields, SLOTS)):
            place = jnp.where(lane_ids == slot + shift, 1.0, 0.0).astype(BF16)
            left = spread_parts(jnp.concatenate([fields, fields], axis=0), hit)
            total = total + dot(left, place, NT)
    total = sum_parts(total).reshape(pairs, 4, 4 * SLOTS)
    out_ref[:, 0:4, :] = total[:, :, : 2 * SLOTS]
    out_ref[:, 4:8, :] = total[:, :, 2 * SLOTS :]


def spread_parts(fields, hit):
    rows = hit.shape[0]
    out = []
    for part in split_three(fields):
        wide = part.astype(F32)
        wide = jnp.broadcast_to(wide[None], (rows // 8, 8, 256)).reshape(rows, 256)
        out.append(jnp.where(hit, wide, 0.0).astype(BF16))
    return jnp.concatenate(out, axis=0)


def sum_parts(total):
    rows = total.shape[0] // 3
    return (total[:rows] + total[rows : 2 * rows]) + total[2 * rows :]


def sort_kernel(in_ref, out_ref, fields_ref):
    pairs = in_ref.shape[0]
    blocks = out_ref.shape[0] - 1
    lane = lax.broadcasted_iota(jnp.int32, (4, 128), 1)
    for pair in range(pairs):
        first = in_ref[pair, 0:4, :]
        second = in_ref[pair, 4:8, :]
        low = jnp.where(lane < SLOTS, first, pltpu.roll(second, SLOTS, 1))
        high = jnp.where(lane < SLOTS, pltpu.roll(first, SLOTS, 1), second)
        fields_ref[:, 128 * pair : 128 * (pair + 1)] = jnp.concatenate([low, high], axis=0)
    width = pairs * 128
    tri = strict_upper(256)
    ids = lax.broadcasted_iota(jnp.int32, (16, 256), 0) + 1
    count = jnp.zeros((16, 256), F32)
    for start in range(0, width, 256):
        key = fields_ref[0:1, start : start + 256].astype(jnp.int32)
        count = count + jnp.where(key == ids, 1.0, 0.0)
    count = jnp.sum(count, axis=1, keepdims=True).astype(jnp.int32)
    used = ((count + (TILE - 1)) >> 7).astype(F32)
    rows = lax.broadcasted_iota(jnp.int32, (16, 16), 0)
    columns = lax.broadcasted_iota(jnp.int32, (16, 16), 1)
    before = jnp.where(columns < rows, 1.0, 0.0).astype(BF16)
    first_tile = dot(before, jnp.broadcast_to(used, (16, 128)).astype(BF16))[:, 0:1]
    tile_ids = lax.broadcasted_iota(jnp.int32, (blocks * 8, 256), 0) >> 3
    lane_ids = lax.broadcasted_iota(jnp.int32, (256, 256), 0)
    carry = first_tile * TILE
    total = jnp.zeros((blocks * 8 * 3, 256), F32)
    for start in range(0, width, 256):
        fields = fields_ref[:, start : start + 256]
        key = fields[0:1].astype(jnp.int32)
        mark = jnp.where(key == ids, 1.0, 0.0)
        ahead = dot(mark.astype(BF16), tri) + carry
        carry = carry + jnp.sum(mark, axis=1, keepdims=True)
        spot = jnp.sum(mark * ahead, axis=0, keepdims=True).astype(jnp.int32)
        spot = jnp.where(key >= 1, spot, -1)
        hit = tile_ids == (spot >> 8)
        place = jnp.where(lane_ids == (spot & 255), 1.0, 0.0).astype(BF16)
        total = total + dot(spread_parts(fields, hit), place, NT)
    out_ref[0:blocks] = sum_parts(total).reshape(blocks, 8, 256)
    lane = lax.broadcasted_iota(jnp.int32, (16, 256), 1).astype(F32)
    box = jnp.sum(jnp.where(first_tile + used <= lane, 1.0, 0.0), axis=0, keepdims=True)
    in_use = (jnp.sum(used, axis=0, keepdims=True).astype(jnp.int32) + 1) >> 1
    row = lax.broadcasted_iota(jnp.int32, (8, 256), 0)
    out_ref[blocks] = jnp.where(row == 0, box, in_use.astype(F32))


LEAF_STEP = 4
IMAGE_STEP = 8


def add_samples(fields_refs, leaf_ref, circle_ref, facts_ref, sems):
    blocks = fields_refs[0].shape[0] - 1
    quads = range(len(fields_refs))

    def fact(index, row, lane):
        return facts_ref[index, row, lane].astype(jnp.int32)

    def make_weights(fields):
        first_axis = lagrange_rows(fields[1:2])
        second_axis = lagrange_rows(fields[2:3])
        rows = []
        for part in range(2):
            scaled = second_axis * fields[5 + part : 6 + part]
            rows += [first_axis[k : k + 1] * scaled for k in range(8)]
        return split_two(jnp.concatenate(rows, axis=0))

    def make_waves(fields):
        cosines = []
        sines = []
        for row in range(0, 256, 32):
            across = circle_ref[0, row : row + 32]
            along = circle_ref[1, row : row + 32]
            turns = (
                jnp.concatenate([across, across], axis=1) * fields[3:4]
                + jnp.concatenate([along, along], axis=1) * fields[4:5]
            )
            cosine, sine = cos_sin_turns(turns)
            cosines.append(split_two(cosine))
            sines.append(split_two(sine))
        return [jnp.concatenate([v[k] for v in cosines + sines], axis=0) for k in range(2)]

    def accumulate(index, box, waves, weights):
        high, low = weights
        right = jnp.concatenate(
            [
                jnp.concatenate([high, high], axis=1),
                jnp.concatenate([low, jnp.zeros_like(low)], axis=1),
            ],
            axis=0,
        )
        total = dot(jnp.concatenate(waves, axis=1), right, NT)
        leaf_ref[index, box] += total[:, 0:128] + total[:, 128:256]

    copies = [
        pltpu.make_async_copy(fields_refs[index].at[blocks], facts_ref.at[index], sems.at[index])
        for index in quads
    ]
    for copy in copies:
        copy.start()
    target = lax.broadcasted_iota(jnp.int32, (256, 128), 0).astype(F32)
    for k, value in enumerate(cos_sin_turns(target * (1.0 / 512.0))):
        circle_ref[k] = value * np.float32(WAVENUMBER / (2.0 * np.pi))

    @pl.loop(0, len(fields_refs))
    def _(index):
        @pl.loop(0, leaf_ref.shape[1])
        def _(box):
            leaf_ref[index, box] = jnp.zeros_like(leaf_ref[index, box])

    for copy in copies:
        copy.wait()
    steps = fact(0, 1, 0)
    for index in quads[1:]:
        steps = jnp.maximum(steps, fact(index, 1, 0))
    stride = 2 if len(quads) == 1 else 1

    @pl.loop(0, (steps + (stride - 1)) // stride)
    def _(step):
        for index, ahead in [(index, ahead) for index in quads for ahead in range(stride)]:
            block = step * stride + ahead
            fields = fields_refs[index][block]
            waves = make_waves(fields)
            weights = make_weights(fields)
            for k in range(2):
                lanes = slice(TILE * k, TILE * (k + 1))
                accumulate(
                    index,
                    fact(index, 0, 2 * block + k),
                    [half[:, lanes] for half in waves],
                    [half[:, lanes] for half in weights],
                )


def leaf_scratch(count):
    return [
        pltpu.VMEM((2, 256, 128), F32),
        pltpu.SMEM((count, 8, 2 * TILE), F32),
        pltpu.SemaphoreType.DMA((count,)),
    ]


def own_leaf_kernel(fields_ref, leaf_ref, token_ref, circle_ref, facts_ref, sems):
    token_ref[...] = jnp.zeros_like(token_ref)
    add_samples([fields_ref], leaf_ref, circle_ref, facts_ref, sems)


def leaf_kernel(bits_ref, *refs):
    fields_refs = refs[:3]
    own_leaf_ref, one_ref, two_ref, turn_ref = refs[3:7]
    partner_ref, own_ref, leaf_ref, circle_ref, facts_ref, sems = refs[8:]
    add_samples(fields_refs, leaf_ref, circle_ref, facts_ref, sems)
    leaves = [own_leaf_ref.at[0], leaf_ref.at[0], leaf_ref.at[1], leaf_ref.at[2]]
    low_bit = bits_ref[0]
    high_bit = bits_ref[1]
    matrix = jnp.concatenate([one_ref[low_bit, low_bit], one_ref[1 - low_bit, low_bit]], axis=1)
    second = stacked_halves(two_ref[high_bit, high_bit])
    sign = jnp.where(lax.broadcasted_iota(jnp.int32, (256, 128), 1) < 64, -1.0, 1.0)

    def first_level(index, box):
        parts = []
        for child in (index, index + 1):
            even = leaves[child][box, 0:256]
            odd = pltpu.roll(leaves[child][box, 256:512], 64, 1) * sign
            parts.append(jnp.concatenate([even + odd, even - odd], axis=0))
        return deep_product(matrix, jnp.concatenate(parts, axis=1))

    @pl.loop(0, turn_ref.shape[1], step=LEAF_STEP)
    def _(begin):
        owns = {}
        for k in range(LEAF_STEP + 1):
            if k < LEAF_STEP:
                owns[k] = first_level(0, begin + k)
                partner_ref[begin + k] = first_level(2, begin + k)
            if k > 0:
                turned = rotate_by(owns[k - 1], *[turn_ref[h, begin + k - 1] for h in range(2)])
                own_ref[begin + k - 1] = product_128(second, turned)


def turn_kernel(one_ref, two_ref, one_out, two_out):
    for angle_ref, out in ((one_ref, one_out), (two_ref, two_out)):
        for k in range(angle_ref.shape[0]):
            out[0, k], out[1, k] = cos_sin(angle_ref[k] * np.float32(0.5 / np.pi))


def rotate(coef, angle):
    return rotate_by(coef, *cos_sin(angle * np.float32(0.5 / np.pi)))


def rotate_by(coef, cosine, sine):
    real_part = coef[:64]
    imag_part = coef[64:]
    return jnp.concatenate(
        [cosine * real_part - sine * imag_part, sine * real_part + cosine * imag_part], axis=0
    )


def image_kernel(
    bits_ref, partner_ref, own_ref, early_ref, late_ref, two_ref, matrix_ref, pixel_ref, out_ref
):
    high_bit = bits_ref[1]
    matrix = stacked_halves(matrix_ref[1 - high_bit, high_bit])
    pixel = stacked_halves(pixel_ref[...])
    early = early_ref.shape[0]
    seconds = {}
    images = {}
    begin = pl.program_id(0) * IMAGE_STEP
    for k in range(IMAGE_STEP + 2):
        if k < IMAGE_STEP:
            box = begin + k
            phase = jnp.where(
                box < early,
                early_ref[jnp.minimum(box, early - 1)],
                late_ref[jnp.maximum(box - early, 0)],
            )
            first = rotate(partner_ref[box], phase)
            seconds[k] = own_ref[box] + product_128(matrix, first)
        if 1 <= k <= IMAGE_STEP:
            turned = rotate_by(
                seconds[k - 1], *[two_ref[h, begin + k - 1] for h in range(2)]
            )
            images[k - 1] = product_128(pixel, turned)
        if k >= 2:
            out_ref[k - 2] = images[k - 2]


KEPT = pl.BlockSpec(memory_space=pltpu.VMEM)


def whole(shape):
    return pl.BlockSpec(shape, lambda *_: (0,) * len(shape))


def params(mebibytes=24):
    return pltpu.CompilerParams(vmem_limit_bytes=mebibytes * 1024 * 1024)


def from_quad(value, mask):
    pairs = [(source, source ^ mask) for source in range(lax.axis_size("quad"))]
    return lax.ppermute(value, "quad", pairs)


def body(sample_box, sample_coords, sample_values, level_one, level_two, phase_one, phase_two):
    senders = lax.axis_size("box")
    boxes = phase_one.shape[1]
    targets = phase_one.shape[3]
    early = EARLY
    phase_one = phase_one[0]
    phase_two = phase_two[0]

    early_shape = (early,) + phase_one.shape[1:]
    late_shape = (boxes - early,) + phase_one.shape[1:]
    sample_box = sample_box.reshape(1, -1)
    packed_shape = (senders // 2, 8, 128)
    operands = (sample_box, sample_coords, sample_values, phase_one)
    results = (packed_shape, early_shape, late_shape)
    packed, early_source, late_source = pl.pallas_call(
        pack_kernel,
        grid=(1,),
        in_specs=[whole(v.shape) for v in operands],
        out_specs=[whole(v) for v in results],
        out_shape=[jax.ShapeDtypeStruct(v, F32) for v in results],
        compiler_params=params(60),
        name="pack",
    )(*operands)
    early_phase = from_quad(early_source, 2)
    arrived = lax.all_to_all(
        packed.reshape(senders, 4, 128), "box", split_axis=0, concat_axis=0, tiled=True
    )
    arrived, early_phase = lax.optimization_barrier((arrived, early_phase))
    ordered = pl.pallas_call(
        sort_kernel,
        out_shape=jax.ShapeDtypeStruct((BLOCKS + 1, 8, 2 * TILE), F32),
        scratch_shapes=[pltpu.VMEM((8, senders * SLOTS), F32)],
        compiler_params=params(),
        name="sort",
    )(arrived.reshape(senders // 2, 8, 128))
    others = [from_quad(ordered, mask) for mask in (1, 2, 3)]

    quad_index = lax.axis_index("quad")
    bits = jnp.stack([quad_index % 2, quad_index // 2])

    turn_in = pl.BlockSpec((4,) + phase_one.shape[1:], lambda b: (b, 0, 0))
    turn_out = pl.BlockSpec((2, 4) + phase_one.shape[1:], lambda b: (0, b, 0, 0))
    turn_one, turn_two = pl.pallas_call(
        turn_kernel,
        grid=(boxes // 4,),
        in_specs=[turn_in] * 2,
        out_specs=[turn_out] * 2,
        out_shape=[jax.ShapeDtypeStruct((2,) + phase_one.shape, F32)] * 2,
        compiler_params=params(60),
        name="turn",
    )(phase_one, phase_two)

    scalars = pl.BlockSpec(memory_space=pltpu.SMEM)
    own_leaf, token = pl.pallas_call(
        own_leaf_kernel,
        in_specs=[KEPT],
        out_specs=[KEPT] * 2,
        out_shape=[
            jax.ShapeDtypeStruct((1, boxes + 1, 512, 128), F32),
            jax.ShapeDtypeStruct((8, 128), F32),
        ],
        scratch_shapes=leaf_scratch(1),
        compiler_params=params(24),
        cost_estimate=pl.CostEstimate(flops=9 * 10**9, bytes_accessed=8 * 10**6, transcendentals=0),
        name="own_leaf",
    )(ordered)
    late_source, token = lax.optimization_barrier((late_source, token))
    late_phase = from_quad(late_source, 2)
    partner, own = pl.pallas_call(
        leaf_kernel,
        in_specs=[scalars] + [KEPT] * 8,
        out_specs=[KEPT] * 2,
        out_shape=[jax.ShapeDtypeStruct((boxes, 128, targets), F32)] * 2,
        scratch_shapes=[pltpu.VMEM((3, boxes + 1, 512, 128), F32)] + leaf_scratch(3),
        compiler_params=params(32),
        cost_estimate=pl.CostEstimate(flops=30 * 10**9, bytes_accessed=24 * 10**6, transcendentals=0),
        name="leaf",
    )(bits, *others, own_leaf, level_one, level_two, turn_one, token)

    pixel = jnp.asarray(pixel_matrix())

    image = pl.pallas_call(
        image_kernel,
        grid=(boxes // IMAGE_STEP,),
        in_specs=[scalars] + [KEPT] * 7,
        out_specs=pl.BlockSpec((IMAGE_STEP, 128, targets), lambda b: (b, 0, 0)),
        out_shape=jax.ShapeDtypeStruct((boxes, 128, targets), F32),
        compiler_params=params(24),
        name="image",
    )(bits, partner, own, early_phase, late_phase, turn_two, level_two, pixel)
    return image[None]


def solution(mesh):
    placed = (
        P(("quad", "box")),
        P(None, ("quad", "box")),
        P(None, ("quad", "box")),
        P(),
        P(),
        P("quad", "box", None, None),
        P("quad", "box", None, None),
    )
    return jax.shard_map(
        body, mesh=mesh, in_specs=placed, out_specs=P("quad", "box", None, None), check_vma=False
    )
```

```python
import functools

import jax
import jax.numpy as jnp
import numpy as np
from jax import lax
from jax.experimental import pallas as pl
from jax.experimental.pallas import tpu as pltpu
from jax.sharding import PartitionSpec as P

WAVENUMBER = 6.0
SLOTS = 64
TILE = 128
BLOCKS = 24
EARLY = 6

F32 = jnp.float32
BF16 = jnp.bfloat16
NN = (((1,), (0,)), ((), ()))
NT = (((1,), (1,)), ((), ()))


def node_table():
    nodes = np.cos(np.pi * (2.0 * np.arange(8) + 1.0) / 16.0)
    scales = []
    for center in range(8):
        product = 1.0
        for other_node in range(8):
            if other_node != center:
                product = product * (nodes[center] - nodes[other_node])
        scales.append(1.0 / product)
    return ([float(v) for v in nodes], scales)


def lagrange_rows(points):
    nodes, scales = node_table()
    row = lax.broadcasted_iota(jnp.int32, (8, points.shape[1]), 0)
    factor = None
    for node in range(8):
        term = jnp.where(row == node, scales[node], points - nodes[node])
        factor = term if factor is None else factor * term
    return factor


def pixel_matrix():
    nodes, scales = node_table()
    pixels = -1.0 + (2.0 * np.arange(8) + 1.0) / 8.0
    weights = np.zeros((8, 8))
    for center in range(8):
        value = np.full(8, scales[center])
        for other_node in range(8):
            if other_node != center:
                value = value * (pixels - nodes[other_node])
        weights[center] = value
    one_part = np.einsum("ki,mj->ijkm", weights, weights).reshape(64, 64)
    return np.kron(np.eye(2), one_part).astype(np.float32)


def series(function, limit, terms):
    grid = 0.5 * limit * limit * (1.0 - np.cos(np.pi * (np.arange(400) + 0.5) / 400))
    values = function(np.sqrt(grid))
    fit = np.polynomial.chebyshev.Chebyshev.fit(grid, values, terms - 1, domain=[0, limit * limit])
    return [float(v) for v in fit.convert(kind=np.polynomial.Polynomial).coef]


def horner(coefs, square):
    total = coefs[-1]
    for coef in coefs[-2::-1]:
        total = total * square + coef
    return total


def cos_sin(half_turns):
    square = half_turns * half_turns
    sine = horner(SINE, square) * half_turns
    cosine = horner(COSINE, square)
    twice = sine + sine
    return 1.0 - twice * sine, twice * cosine


SINE = series(lambda x: np.pi * np.sinc(x), 0.5001, 5)
COSINE = series(lambda x: np.cos(np.pi * x), 0.5001, 5)
ROUNDER = np.float32(1.5 * 2**23)


def cos_sin_turns(turns):
    return cos_sin(turns - ((turns + ROUNDER) - ROUNDER))


def split_two(value):
    high = value.astype(BF16)
    return high, (value - high.astype(F32)).astype(BF16)


def split_three(value):
    high = value.astype(BF16)
    rest = value - high.astype(F32)
    middle = rest.astype(BF16)
    low = (rest - middle.astype(F32)).astype(BF16)
    return high, middle, low


def dot(left, right, dims=NN):
    return lax.dot_general(left, right, dims, preferred_element_type=F32)


def deep_product(matrix, right):
    high, low = split_two(matrix)
    right_high, right_low = split_two(right)
    both = dot(jnp.concatenate([high, low], axis=0), right_high, NT)
    return both[:128] + (both[128:] + dot(high, right_low, NT))


def stacked_halves(matrix):
    high, low = split_two(matrix)
    top = jnp.concatenate([high, high], axis=1)
    bottom = jnp.concatenate([low, jnp.zeros_like(low)], axis=1)
    return jnp.concatenate([top, bottom], axis=0)


def product_128(stacked, right):
    both = dot(stacked, jnp.concatenate(split_two(right), axis=0))
    return both[:128] + both[128:]


def strict_upper(size):
    rows = lax.broadcasted_iota(jnp.int32, (size, size), 0)
    columns = lax.broadcasted_iota(jnp.int32, (size, size), 1)
    return jnp.where(rows < columns, 1.0, 0.0).astype(BF16)


def pack_kernel(
    box_ref, coords_ref, values_ref, phase_ref, out_ref, early_ref, late_ref, stage_ref, sems
):
    early = early_ref.shape[0]
    late = late_ref.shape[0]
    fetch = pltpu.make_async_copy(phase_ref, stage_ref, sems.at[0])
    parts = [
        pltpu.make_async_copy(stage_ref.at[pl.ds(0, early)], early_ref, sems.at[1]),
        pltpu.make_async_copy(stage_ref.at[pl.ds(early, late)], late_ref, sems.at[2]),
    ]
    fetch.start()
    pairs = out_ref.shape[0]
    rows = box_ref.shape[1]
    tri = strict_upper(256)
    owner_ids = lax.broadcasted_iota(jnp.int32, (2 * pairs, 256), 0)
    row_pair = lax.broadcasted_iota(jnp.int32, (pairs * 4, 256), 0) >> 2
    lane_ids = lax.broadcasted_iota(jnp.int32, (4 * SLOTS, 256), 0)
    carry = jnp.zeros((2 * pairs, 1), F32)
    total = jnp.zeros((pairs * 4 * 3, 4 * SLOTS), F32)
    for start in range(0, rows, 256):
        if start == rows // 2:
            fetch.wait()
            for copy in parts:
                copy.start()
        box = box_ref[:, start : start + 256]
        owner = box >> 4
        mark = jnp.where(owner_ids == owner, 1.0, 0.0)
        ahead = dot(mark.astype(BF16), tri) + carry
        carry = carry + jnp.sum(mark, axis=1, keepdims=True)
        slot = jnp.sum(mark * ahead, axis=0, keepdims=True).astype(jnp.int32)
        slot = slot + (owner & 1) * (2 * SLOTS)
        key = ((box & 15) + 1).astype(F32)
        coords = coords_ref[:, start : start + 256]
        values = values_ref[:, start : start + 256]
        empty = jnp.zeros_like(key)
        low_fields = jnp.concatenate([key, coords[0:3]], axis=0)
        high_fields = jnp.concatenate([coords[3:4], values, empty], axis=0)
        hit = row_pair == (owner >> 1)
        for fields, shift in ((low_fields, 0), (high_fields, SLOTS)):
            place = jnp.where(lane_ids == slot + shift, 1.0, 0.0).astype(BF16)
            left = spread_parts(jnp.concatenate([fields, fields], axis=0), hit)
            total = total + dot(left, place, NT)
    total = sum_parts(total).reshape(pairs, 4, 4 * SLOTS)
    out_ref[:, 0:4, :] = total[:, :, : 2 * SLOTS]
    out_ref[:, 4:8, :] = total[:, :, 2 * SLOTS :]
    for copy in parts:
        copy.wait()


def spread_parts(fields, hit):
    rows = hit.shape[0]
    out = []
    for part in split_three(fields):
        wide = part.astype(F32)
        wide = jnp.broadcast_to(wide[None], (rows // 8, 8, 256)).reshape(rows, 256)
        out.append(jnp.where(hit, wide, 0.0).astype(BF16))
    return jnp.concatenate(out, axis=0)


def sum_parts(total):
    rows = total.shape[0] // 3
    return (total[:rows] + total[rows : 2 * rows]) + total[2 * rows :]


def sort_kernel(in_ref, out_ref, fields_ref):
    pairs = in_ref.shape[0]
    blocks = out_ref.shape[0] - 1
    lane = lax.broadcasted_iota(jnp.int32, (4, 128), 1)
    for pair in range(pairs):
        first = in_ref[pair, 0:4, :]
        second = in_ref[pair, 4:8, :]
        low = jnp.where(lane < SLOTS, first, pltpu.roll(second, SLOTS, 1))
        high = jnp.where(lane < SLOTS, pltpu.roll(first, SLOTS, 1), second)
        fields_ref[:, 128 * pair : 128 * (pair + 1)] = jnp.concatenate([low, high], axis=0)
    width = pairs * 128
    tri = strict_upper(256)
    ids = lax.broadcasted_iota(jnp.int32, (16, 256), 0) + 1
    count = jnp.zeros((16, 256), F32)
    for start in range(0, width, 256):
        key = fields_ref[0:1, start : start + 256].astype(jnp.int32)
        count = count + jnp.where(key == ids, 1.0, 0.0)
    count = jnp.sum(count, axis=1, keepdims=True).astype(jnp.int32)
    used = ((count + (TILE - 1)) >> 7).astype(F32)
    rows = lax.broadcasted_iota(jnp.int32, (16, 16), 0)
    columns = lax.broadcasted_iota(jnp.int32, (16, 16), 1)
    before = jnp.where(columns < rows, 1.0, 0.0).astype(BF16)
    first_tile = dot(before, jnp.broadcast_to(used, (16, 128)).astype(BF16))[:, 0:1]
    tile_ids = lax.broadcasted_iota(jnp.int32, (blocks * 8, 256), 0) >> 3
    lane_ids = lax.broadcasted_iota(jnp.int32, (256, 256), 0)
    carry = first_tile * TILE
    total = jnp.zeros((blocks * 8 * 3, 256), F32)
    for start in range(0, width, 256):
        fields = fields_ref[:, start : start + 256]
        key = fields[0:1].astype(jnp.int32)
        mark = jnp.where(key == ids, 1.0, 0.0)
        ahead = dot(mark.astype(BF16), tri) + carry
        carry = carry + jnp.sum(mark, axis=1, keepdims=True)
        spot = jnp.sum(mark * ahead, axis=0, keepdims=True).astype(jnp.int32)
        spot = jnp.where(key >= 1, spot, -1)
        hit = tile_ids == (spot >> 8)
        place = jnp.where(lane_ids == (spot & 255), 1.0, 0.0).astype(BF16)
        total = total + dot(spread_parts(fields, hit), place, NT)
    out_ref[0:blocks] = sum_parts(total).reshape(blocks, 8, 256)
    lane = lax.broadcasted_iota(jnp.int32, (16, 256), 1).astype(F32)
    box = jnp.sum(jnp.where(first_tile + used <= lane, 1.0, 0.0), axis=0, keepdims=True)
    in_use = (jnp.sum(used, axis=0, keepdims=True).astype(jnp.int32) + 1) >> 1
    row = lax.broadcasted_iota(jnp.int32, (8, 256), 0)
    out_ref[blocks] = jnp.where(row == 0, box, in_use.astype(F32))


LEAF_STEP = 4
IMAGE_STEP = 8


def add_samples(fields_refs, leaf_ref, circle_ref, facts_ref, sems):
    blocks = fields_refs[0].shape[0] - 1
    quads = range(len(fields_refs))

    def fact(index, row, lane):
        return facts_ref[index, row, lane].astype(jnp.int32)

    def make_weights(fields):
        first_axis = lagrange_rows(fields[1:2])
        second_axis = lagrange_rows(fields[2:3])
        rows = []
        for part in range(2):
            scaled = second_axis * fields[5 + part : 6 + part]
            rows += [first_axis[k : k + 1] * scaled for k in range(8)]
        return split_two(jnp.concatenate(rows, axis=0))

    def make_waves(fields):
        cosines = []
        sines = []
        for row in range(0, 256, 32):
            across = circle_ref[0, row : row + 32]
            along = circle_ref[1, row : row + 32]
            turns = (
                jnp.concatenate([across, across], axis=1) * fields[3:4]
                + jnp.concatenate([along, along], axis=1) * fields[4:5]
            )
            cosine, sine = cos_sin_turns(turns)
            cosines.append(split_two(cosine))
            sines.append(split_two(sine))
        return [jnp.concatenate([v[k] for v in cosines + sines], axis=0) for k in range(2)]

    def accumulate(index, box, waves, weights):
        high, low = weights
        right = jnp.concatenate(
            [
                jnp.concatenate([high, high], axis=1),
                jnp.concatenate([low, jnp.zeros_like(low)], axis=1),
            ],
            axis=0,
        )
        total = dot(jnp.concatenate(waves, axis=1), right, NT)
        leaf_ref[index, box] += total[:, 0:128] + total[:, 128:256]

    copies = [
        pltpu.make_async_copy(fields_refs[index].at[blocks], facts_ref.at[index], sems.at[index])
        for index in quads
    ]
    for copy in copies:
        copy.start()
    target = lax.broadcasted_iota(jnp.int32, (256, 128), 0).astype(F32)
    for k, value in enumerate(cos_sin_turns(target * (1.0 / 512.0))):
        circle_ref[k] = value * np.float32(WAVENUMBER / (2.0 * np.pi))

    @pl.loop(0, len(fields_refs))
    def _(index):
        @pl.loop(0, leaf_ref.shape[1])
        def _(box):
            leaf_ref[index, box] = jnp.zeros_like(leaf_ref[index, box])

    for copy in copies:
        copy.wait()
    steps = fact(0, 1, 0)
    for index in quads[1:]:
        steps = jnp.maximum(steps, fact(index, 1, 0))
    stride = 2 if len(quads) == 1 else 1

    @pl.loop(0, (steps + (stride - 1)) // stride)
    def _(step):
        for index, ahead in [(index, ahead) for index in quads for ahead in range(stride)]:
            block = step * stride + ahead
            fields = fields_refs[index][block]
            waves = make_waves(fields)
            weights = make_weights(fields)
            for k in range(2):
                lanes = slice(TILE * k, TILE * (k + 1))
                accumulate(
                    index,
                    fact(index, 0, 2 * block + k),
                    [half[:, lanes] for half in waves],
                    [half[:, lanes] for half in weights],
                )


def leaf_scratch(count):
    return [
        pltpu.VMEM((2, 256, 128), F32),
        pltpu.SMEM((count, 8, 2 * TILE), F32),
        pltpu.SemaphoreType.DMA((count,)),
    ]


def own_leaf_kernel(fields_ref, leaf_ref, token_ref, circle_ref, facts_ref, sems):
    token_ref[...] = jnp.zeros_like(token_ref)
    add_samples([fields_ref], leaf_ref, circle_ref, facts_ref, sems)


def leaf_kernel(bits_ref, *refs):
    fields_refs = refs[:3]
    own_leaf_ref, one_ref, two_ref, turn_ref = refs[3:7]
    partner_ref, own_ref, leaf_ref, circle_ref, facts_ref, sems = refs[8:]
    add_samples(fields_refs, leaf_ref, circle_ref, facts_ref, sems)
    leaves = [own_leaf_ref.at[0], leaf_ref.at[0], leaf_ref.at[1], leaf_ref.at[2]]
    low_bit = bits_ref[0]
    high_bit = bits_ref[1]
    matrix = jnp.concatenate([one_ref[low_bit, low_bit], one_ref[1 - low_bit, low_bit]], axis=1)
    second = stacked_halves(two_ref[high_bit, high_bit])
    sign = jnp.where(lax.broadcasted_iota(jnp.int32, (256, 128), 1) < 64, -1.0, 1.0)

    def first_level(index, box):
        parts = []
        for child in (index, index + 1):
            even = leaves[child][box, 0:256]
            odd = pltpu.roll(leaves[child][box, 256:512], 64, 1) * sign
            parts.append(jnp.concatenate([even + odd, even - odd], axis=0))
        return deep_product(matrix, jnp.concatenate(parts, axis=1))

    @pl.loop(0, turn_ref.shape[1], step=LEAF_STEP)
    def _(begin):
        owns = {}
        for k in range(LEAF_STEP + 1):
            if k < LEAF_STEP:
                owns[k] = first_level(0, begin + k)
                partner_ref[begin + k] = first_level(2, begin + k)
            if k > 0:
                turned = rotate_by(owns[k - 1], *[turn_ref[h, begin + k - 1] for h in range(2)])
                own_ref[begin + k - 1] = product_128(second, turned)


def turn_kernel(one_ref, two_ref, one_out, two_out):
    for angle_ref, out in ((one_ref, one_out), (two_ref, two_out)):
        for k in range(angle_ref.shape[0]):
            out[0, k], out[1, k] = cos_sin(angle_ref[k] * np.float32(0.5 / np.pi))


def rotate(coef, angle):
    return rotate_by(coef, *cos_sin(angle * np.float32(0.5 / np.pi)))


def rotate_by(coef, cosine, sine):
    real_part = coef[:64]
    imag_part = coef[64:]
    return jnp.concatenate(
        [cosine * real_part - sine * imag_part, sine * real_part + cosine * imag_part], axis=0
    )


def image_kernel(
    bits_ref, partner_ref, own_ref, early_ref, late_ref, two_ref, matrix_ref, pixel_ref, out_ref
):
    high_bit = bits_ref[1]
    matrix = stacked_halves(matrix_ref[1 - high_bit, high_bit])
    pixel = stacked_halves(pixel_ref[...])
    early = early_ref.shape[0]
    seconds = {}
    images = {}
    begin = pl.program_id(0) * IMAGE_STEP
    for k in range(IMAGE_STEP + 2):
        if k < IMAGE_STEP:
            box = begin + k
            phase = jnp.where(
                box < early,
                early_ref[jnp.minimum(box, early - 1)],
                late_ref[jnp.maximum(box - early, 0)],
            )
            first = rotate(partner_ref[box], phase)
            seconds[k] = own_ref[box] + product_128(matrix, first)
        if 1 <= k <= IMAGE_STEP:
            turned = rotate_by(
                seconds[k - 1], *[two_ref[h, begin + k - 1] for h in range(2)]
            )
            images[k - 1] = product_128(pixel, turned)
        if k >= 2:
            out_ref[k - 2] = images[k - 2]


KEPT = pl.BlockSpec(memory_space=pltpu.VMEM)


def whole(shape):
    return pl.BlockSpec(shape, lambda *_: (0,) * len(shape))


def params(mebibytes=24):
    return pltpu.CompilerParams(vmem_limit_bytes=mebibytes * 1024 * 1024)


def from_quad(value, mask):
    pairs = [(source, source ^ mask) for source in range(lax.axis_size("quad"))]
    return lax.ppermute(value, "quad", pairs)


def body(sample_box, sample_coords, sample_values, level_one, level_two, phase_one, phase_two):
    senders = lax.axis_size("box")
    boxes = phase_one.shape[1]
    targets = phase_one.shape[3]
    early = EARLY
    phase_one = phase_one[0]
    phase_two = phase_two[0]

    early_shape = (early,) + phase_one.shape[1:]
    late_shape = (boxes - early,) + phase_one.shape[1:]
    sample_box = sample_box.reshape(1, -1)
    packed_shape = (senders // 2, 8, 128)
    operands = (sample_box, sample_coords, sample_values, phase_one)
    results = (packed_shape, early_shape, late_shape)
    packed, early_source, late_source = pl.pallas_call(
        pack_kernel,
        grid=(1,),
        in_specs=[whole(v.shape) for v in operands[:3]] + [pl.BlockSpec(memory_space=pl.ANY)],
        out_specs=[whole(packed_shape)] + [pl.BlockSpec(memory_space=pl.ANY)] * 2,
        out_shape=[jax.ShapeDtypeStruct(v, F32) for v in results],
        scratch_shapes=[pltpu.VMEM(phase_one.shape, F32), pltpu.SemaphoreType.DMA((3,))],
        compiler_params=params(60),
        name="pack",
    )(*operands)
    early_phase = from_quad(early_source, 2)
    arrived = lax.all_to_all(
        packed.reshape(senders, 4, 128), "box", split_axis=0, concat_axis=0, tiled=True
    )
    arrived, early_phase = lax.optimization_barrier((arrived, early_phase))
    ordered = pl.pallas_call(
        sort_kernel,
        out_shape=jax.ShapeDtypeStruct((BLOCKS + 1, 8, 2 * TILE), F32),
        scratch_shapes=[pltpu.VMEM((8, senders * SLOTS), F32)],
        compiler_params=params(),
        name="sort",
    )(arrived.reshape(senders // 2, 8, 128))
    others = [from_quad(ordered, mask) for mask in (1, 2, 3)]

    quad_index = lax.axis_index("quad")
    bits = jnp.stack([quad_index % 2, quad_index // 2])

    turn_in = pl.BlockSpec((4,) + phase_one.shape[1:], lambda b: (b, 0, 0))
    turn_out = pl.BlockSpec((2, 4) + phase_one.shape[1:], lambda b: (0, b, 0, 0))
    turn_one, turn_two = pl.pallas_call(
        turn_kernel,
        grid=(boxes // 4,),
        in_specs=[turn_in] * 2,
        out_specs=[turn_out] * 2,
        out_shape=[jax.ShapeDtypeStruct((2,) + phase_one.shape, F32)] * 2,
        compiler_params=params(60),
        name="turn",
    )(phase_one, phase_two)

    scalars = pl.BlockSpec(memory_space=pltpu.SMEM)
    own_leaf, token = pl.pallas_call(
        own_leaf_kernel,
        in_specs=[KEPT],
        out_specs=[KEPT] * 2,
        out_shape=[
            jax.ShapeDtypeStruct((1, boxes + 1, 512, 128), F32),
            jax.ShapeDtypeStruct((8, 128), F32),
        ],
        scratch_shapes=leaf_scratch(1),
        compiler_params=params(24),
        cost_estimate=pl.CostEstimate(flops=9 * 10**9, bytes_accessed=8 * 10**6, transcendentals=0),
        name="own_leaf",
    )(ordered)
    late_source, token = lax.optimization_barrier((late_source, token))
    late_phase = from_quad(late_source, 2)
    partner, own = pl.pallas_call(
        leaf_kernel,
        in_specs=[scalars] + [KEPT] * 8,
        out_specs=[KEPT] * 2,
        out_shape=[jax.ShapeDtypeStruct((boxes, 128, targets), F32)] * 2,
        scratch_shapes=[pltpu.VMEM((3, boxes + 1, 512, 128), F32)] + leaf_scratch(3),
        compiler_params=params(32),
        cost_estimate=pl.CostEstimate(flops=30 * 10**9, bytes_accessed=24 * 10**6, transcendentals=0),
        name="leaf",
    )(bits, *others, own_leaf, level_one, level_two, turn_one, token)

    pixel = jnp.asarray(pixel_matrix())

    image = pl.pallas_call(
        image_kernel,
        grid=(boxes // IMAGE_STEP,),
        in_specs=[scalars] + [KEPT] * 7,
        out_specs=pl.BlockSpec((IMAGE_STEP, 128, targets), lambda b: (b, 0, 0)),
        out_shape=jax.ShapeDtypeStruct((boxes, 128, targets), F32),
        compiler_params=params(24),
        name="image",
    )(bits, partner, own, early_phase, late_phase, turn_two, level_two, pixel)
    return image[None]


def solution(mesh):
    placed = (
        P(("quad", "box")),
        P(None, ("quad", "box")),
        P(None, ("quad", "box")),
        P(),
        P(),
        P("quad", "box", None, None),
        P("quad", "box", None, None),
    )
    return jax.shard_map(
        body, mesh=mesh, in_specs=placed, out_specs=P("quad", "box", None, None), check_vma=False
    )
```

```python
import functools

import jax
import jax.numpy as jnp
import numpy as np
from jax import lax
from jax.experimental import pallas as pl
from jax.experimental.pallas import tpu as pltpu
from jax.sharding import PartitionSpec as P

WAVENUMBER = 6.0
SLOTS = 64
TILE = 128
BLOCKS = 24
EARLY = 6

F32 = jnp.float32
BF16 = jnp.bfloat16
NN = (((1,), (0,)), ((), ()))
NT = (((1,), (1,)), ((), ()))


def node_table():
    nodes = np.cos(np.pi * (2.0 * np.arange(8) + 1.0) / 16.0)
    scales = []
    for center in range(8):
        product = 1.0
        for other_node in range(8):
            if other_node != center:
                product = product * (nodes[center] - nodes[other_node])
        scales.append(1.0 / product)
    return ([float(v) for v in nodes], scales)


def lagrange_rows(points):
    nodes, scales = node_table()
    row = lax.broadcasted_iota(jnp.int32, (8, points.shape[1]), 0)
    factor = None
    for node in range(8):
        term = jnp.where(row == node, scales[node], points - nodes[node])
        factor = term if factor is None else factor * term
    return factor


def pixel_matrix():
    nodes, scales = node_table()
    pixels = -1.0 + (2.0 * np.arange(8) + 1.0) / 8.0
    weights = np.zeros((8, 8))
    for center in range(8):
        value = np.full(8, scales[center])
        for other_node in range(8):
            if other_node != center:
                value = value * (pixels - nodes[other_node])
        weights[center] = value
    one_part = np.einsum("ki,mj->ijkm", weights, weights).reshape(64, 64)
    return np.kron(np.eye(2), one_part).astype(np.float32)


def series(function, limit, terms):
    grid = 0.5 * limit * limit * (1.0 - np.cos(np.pi * (np.arange(400) + 0.5) / 400))
    values = function(np.sqrt(grid))
    fit = np.polynomial.chebyshev.Chebyshev.fit(grid, values, terms - 1, domain=[0, limit * limit])
    return [float(v) for v in fit.convert(kind=np.polynomial.Polynomial).coef]


def horner(coefs, square):
    total = coefs[-1]
    for coef in coefs[-2::-1]:
        total = total * square + coef
    return total


def cos_sin(half_turns):
    square = half_turns * half_turns
    sine = horner(SINE, square) * half_turns
    cosine = horner(COSINE, square)
    twice = sine + sine
    return 1.0 - twice * sine, twice * cosine


SINE = series(lambda x: np.pi * np.sinc(x), 0.5001, 5)
COSINE = series(lambda x: np.cos(np.pi * x), 0.5001, 5)
ROUNDER = np.float32(1.5 * 2**23)


def cos_sin_turns(turns):
    return cos_sin(turns - ((turns + ROUNDER) - ROUNDER))


def split_two(value):
    high = value.astype(BF16)
    return high, (value - high.astype(F32)).astype(BF16)


def split_three(value):
    high = value.astype(BF16)
    rest = value - high.astype(F32)
    middle = rest.astype(BF16)
    low = (rest - middle.astype(F32)).astype(BF16)
    return high, middle, low


def dot(left, right, dims=NN):
    return lax.dot_general(left, right, dims, preferred_element_type=F32)


def deep_product(matrix, right):
    high, low = split_two(matrix)
    right_high, right_low = split_two(right)
    both = dot(jnp.concatenate([high, low], axis=0), right_high, NT)
    return both[:128] + (both[128:] + dot(high, right_low, NT))


def stacked_halves(matrix):
    high, low = split_two(matrix)
    top = jnp.concatenate([high, high], axis=1)
    bottom = jnp.concatenate([low, jnp.zeros_like(low)], axis=1)
    return jnp.concatenate([top, bottom], axis=0)


def product_128(stacked, right):
    both = dot(stacked, jnp.concatenate(split_two(right), axis=0))
    return both[:128] + both[128:]


def strict_upper(size):
    rows = lax.broadcasted_iota(jnp.int32, (size, size), 0)
    columns = lax.broadcasted_iota(jnp.int32, (size, size), 1)
    return jnp.where(rows < columns, 1.0, 0.0).astype(BF16)


def pack_kernel(
    box_ref, coords_ref, values_ref, phase_ref, out_ref, early_ref, late_ref, stage_ref, sems
):
    early = early_ref.shape[0]
    late = late_ref.shape[0]
    fetch = pltpu.make_async_copy(phase_ref, stage_ref, sems.at[0])
    parts = [
        pltpu.make_async_copy(stage_ref.at[pl.ds(0, early)], early_ref, sems.at[1]),
        pltpu.make_async_copy(stage_ref.at[pl.ds(early, late)], late_ref, sems.at[2]),
    ]
    fetch.start()
    pairs = out_ref.shape[0]
    rows = box_ref.shape[1]
    tri = strict_upper(256)
    owner_ids = lax.broadcasted_iota(jnp.int32, (2 * pairs, 256), 0)
    row_pair = lax.broadcasted_iota(jnp.int32, (pairs * 4, 256), 0) >> 2
    lane_ids = lax.broadcasted_iota(jnp.int32, (4 * SLOTS, 256), 0)
    carry = jnp.zeros((2 * pairs, 1), F32)
    total = jnp.zeros((pairs * 4 * 3, 4 * SLOTS), F32)
    for start in range(0, rows, 256):
        if start == rows // 2:
            fetch.wait()
            for copy in parts:
                copy.start()
        box = box_ref[:, start : start + 256]
        owner = box >> 4
        mark = jnp.where(owner_ids == owner, 1.0, 0.0)
        ahead = dot(mark.astype(BF16), tri) + carry
        carry = carry + jnp.sum(mark, axis=1, keepdims=True)
        slot = jnp.sum(mark * ahead, axis=0, keepdims=True).astype(jnp.int32)
        slot = slot + (owner & 1) * (2 * SLOTS)
        key = ((box & 15) + 1).astype(F32)
        coords = coords_ref[:, start : start + 256]
        values = values_ref[:, start : start + 256]
        empty = jnp.zeros_like(key)
        low_fields = jnp.concatenate([key, coords[0:3]], axis=0)
        high_fields = jnp.concatenate([coords[3:4], values, empty], axis=0)
        hit = row_pair == (owner >> 1)
        for fields, shift in ((low_fields, 0), (high_fields, SLOTS)):
            place = jnp.where(lane_ids == slot + shift, 1.0, 0.0).astype(BF16)
            left = spread_parts(jnp.concatenate([fields, fields], axis=0), hit)
            total = total + dot(left, place, NT)
    total = sum_parts(total).reshape(pairs, 4, 4 * SLOTS)
    out_ref[:, 0:4, :] = total[:, :, : 2 * SLOTS]
    out_ref[:, 4:8, :] = total[:, :, 2 * SLOTS :]
    for copy in parts:
        copy.wait()


def spread_parts(fields, hit):
    rows = hit.shape[0]
    out = []
    for part in split_three(fields):
        wide = part.astype(F32)
        wide = jnp.broadcast_to(wide[None], (rows // 8, 8, 256)).reshape(rows, 256)
        out.append(jnp.where(hit, wide, 0.0).astype(BF16))
    return jnp.concatenate(out, axis=0)


def sum_parts(total):
    rows = total.shape[0] // 3
    return (total[:rows] + total[rows : 2 * rows]) + total[2 * rows :]


def sort_kernel(in_ref, out_ref, fields_ref):
    pairs = in_ref.shape[0]
    blocks = out_ref.shape[0] - 1
    lane = lax.broadcasted_iota(jnp.int32, (4, 128), 1)
    for pair in range(pairs):
        first = in_ref[pair, 0:4, :]
        second = in_ref[pair, 4:8, :]
        low = jnp.where(lane < SLOTS, first, pltpu.roll(second, SLOTS, 1))
        high = jnp.where(lane < SLOTS, pltpu.roll(first, SLOTS, 1), second)
        fields_ref[:, 128 * pair : 128 * (pair + 1)] = jnp.concatenate([low, high], axis=0)
    width = pairs * 128
    tri = strict_upper(256)
    ids = lax.broadcasted_iota(jnp.int32, (16, 256), 0) + 1
    count = jnp.zeros((16, 256), F32)
    for start in range(0, width, 256):
        key = fields_ref[0:1, start : start + 256].astype(jnp.int32)
        count = count + jnp.where(key == ids, 1.0, 0.0)
    count = jnp.sum(count, axis=1, keepdims=True).astype(jnp.int32)
    used = ((count + (TILE - 1)) >> 7).astype(F32)
    rows = lax.broadcasted_iota(jnp.int32, (16, 16), 0)
    columns = lax.broadcasted_iota(jnp.int32, (16, 16), 1)
    before = jnp.where(columns < rows, 1.0, 0.0).astype(BF16)
    first_tile = dot(before, jnp.broadcast_to(used, (16, 128)).astype(BF16))[:, 0:1]
    tile_ids = lax.broadcasted_iota(jnp.int32, (blocks * 8, 256), 0) >> 3
    lane_ids = lax.broadcasted_iota(jnp.int32, (256, 256), 0)
    carry = first_tile * TILE
    total = jnp.zeros((blocks * 8 * 3, 256), F32)
    for start in range(0, width, 256):
        fields = fields_ref[:, start : start + 256]
        key = fields[0:1].astype(jnp.int32)
        mark = jnp.where(key == ids, 1.0, 0.0)
        ahead = dot(mark.astype(BF16), tri) + carry
        carry = carry + jnp.sum(mark, axis=1, keepdims=True)
        spot = jnp.sum(mark * ahead, axis=0, keepdims=True).astype(jnp.int32)
        spot = jnp.where(key >= 1, spot, -1)
        hit = tile_ids == (spot >> 8)
        place = jnp.where(lane_ids == (spot & 255), 1.0, 0.0).astype(BF16)
        total = total + dot(spread_parts(fields, hit), place, NT)
    out_ref[0:blocks] = sum_parts(total).reshape(blocks, 8, 256)
    lane = lax.broadcasted_iota(jnp.int32, (16, 256), 1).astype(F32)
    box = jnp.sum(jnp.where(first_tile + used <= lane, 1.0, 0.0), axis=0, keepdims=True)
    in_use = (jnp.sum(used, axis=0, keepdims=True).astype(jnp.int32) + 1) >> 1
    row = lax.broadcasted_iota(jnp.int32, (8, 256), 0)
    out_ref[blocks] = jnp.where(row == 0, box, in_use.astype(F32))


LEAF_STEP = 4
IMAGE_STEP = 8


def add_samples(fields_refs, leaf_ref, circle_ref, facts_ref, sems):
    blocks = fields_refs[0].shape[0] - 1
    quads = range(len(fields_refs))

    def fact(index, row, lane):
        return facts_ref[index, row, lane].astype(jnp.int32)

    def make_weights(fields):
        first_axis = lagrange_rows(fields[1:2])
        second_axis = lagrange_rows(fields[2:3])
        rows = []
        for part in range(2):
            scaled = second_axis * fields[5 + part : 6 + part]
            rows += [first_axis[k : k + 1] * scaled for k in range(8)]
        return split_two(jnp.concatenate(rows, axis=0))

    def make_waves(fields):
        cosines = []
        sines = []
        for row in range(0, 256, 32):
            across = circle_ref[0, row : row + 32]
            along = circle_ref[1, row : row + 32]
            turns = (
                jnp.concatenate([across, across], axis=1) * fields[3:4]
                + jnp.concatenate([along, along], axis=1) * fields[4:5]
            )
            cosine, sine = cos_sin_turns(turns)
            cosines.append(split_two(cosine))
            sines.append(split_two(sine))
        return [jnp.concatenate([v[k] for v in cosines + sines], axis=0) for k in range(2)]

    def accumulate(index, box, waves, weights):
        high, low = weights
        right = jnp.concatenate(
            [
                jnp.concatenate([high, high], axis=1),
                jnp.concatenate([low, jnp.zeros_like(low)], axis=1),
            ],
            axis=0,
        )
        total = dot(jnp.concatenate(waves, axis=1), right, NT)
        leaf_ref[index, box] += total[:, 0:128] + total[:, 128:256]

    copies = [
        pltpu.make_async_copy(fields_refs[index].at[blocks], facts_ref.at[index], sems.at[index])
        for index in quads
    ]
    for copy in copies:
        copy.start()
    target = lax.broadcasted_iota(jnp.int32, (256, 128), 0).astype(F32)
    for k, value in enumerate(cos_sin_turns(target * (1.0 / 512.0))):
        circle_ref[k] = value * np.float32(WAVENUMBER / (2.0 * np.pi))

    @pl.loop(0, len(fields_refs))
    def _(index):
        @pl.loop(0, leaf_ref.shape[1])
        def _(box):
            leaf_ref[index, box] = jnp.zeros_like(leaf_ref[index, box])

    for copy in copies:
        copy.wait()
    steps = fact(0, 1, 0)
    for index in quads[1:]:
        steps = jnp.maximum(steps, fact(index, 1, 0))
    stride = 2 if len(quads) == 1 else 1

    @pl.loop(0, (steps + (stride - 1)) // stride)
    def _(step):
        for index, ahead in [(index, ahead) for index in quads for ahead in range(stride)]:
            block = step * stride + ahead
            fields = fields_refs[index][block]
            waves = make_waves(fields)
            weights = make_weights(fields)
            for k in range(2):
                lanes = slice(TILE * k, TILE * (k + 1))
                accumulate(
                    index,
                    fact(index, 0, 2 * block + k),
                    [half[:, lanes] for half in waves],
                    [half[:, lanes] for half in weights],
                )


def leaf_scratch(count):
    return [
        pltpu.VMEM((2, 256, 128), F32),
        pltpu.SMEM((count, 8, 2 * TILE), F32),
        pltpu.SemaphoreType.DMA((count,)),
    ]


def token_kernel(fields_ref, token_ref):
    token_ref[...] = fields_ref[0, :, 0:128]


def own_leaf_kernel(fields_ref, token_ref, leaf_ref, circle_ref, facts_ref, sems):
    del token_ref
    add_samples([fields_ref], leaf_ref, circle_ref, facts_ref, sems)


def leaf_kernel(bits_ref, *refs):
    fields_refs = refs[:3]
    own_leaf_ref, one_ref, two_ref, turn_ref = refs[3:7]
    partner_ref, own_ref, leaf_ref, circle_ref, facts_ref, sems = refs[7:]
    add_samples(fields_refs, leaf_ref, circle_ref, facts_ref, sems)
    leaves = [own_leaf_ref.at[0], leaf_ref.at[0], leaf_ref.at[1], leaf_ref.at[2]]
    low_bit = bits_ref[0]
    high_bit = bits_ref[1]
    matrix = jnp.concatenate([one_ref[low_bit, low_bit], one_ref[1 - low_bit, low_bit]], axis=1)
    second = stacked_halves(two_ref[high_bit, high_bit])
    sign = jnp.where(lax.broadcasted_iota(jnp.int32, (256, 128), 1) < 64, -1.0, 1.0)

    def first_level(index, box):
        parts = []
        for child in (index, index + 1):
            even = leaves[child][box, 0:256]
            odd = pltpu.roll(leaves[child][box, 256:512], 64, 1) * sign
            parts.append(jnp.concatenate([even + odd, even - odd], axis=0))
        return deep_product(matrix, jnp.concatenate(parts, axis=1))

    @pl.loop(0, turn_ref.shape[1], step=LEAF_STEP)
    def _(begin):
        owns = {}
        for k in range(LEAF_STEP + 1):
            if k < LEAF_STEP:
                owns[k] = first_level(0, begin + k)
                partner_ref[begin + k] = first_level(2, begin + k)
            if k > 0:
                turned = rotate_by(owns[k - 1], *[turn_ref[h, begin + k - 1] for h in range(2)])
                own_ref[begin + k - 1] = product_128(second, turned)


def turn_kernel(one_ref, two_ref, one_out, two_out):
    for angle_ref, out in ((one_ref, one_out), (two_ref, two_out)):
        for k in range(angle_ref.shape[0]):
            out[0, k], out[1, k] = cos_sin(angle_ref[k] * np.float32(0.5 / np.pi))


def rotate(coef, angle):
    return rotate_by(coef, *cos_sin(angle * np.float32(0.5 / np.pi)))


def rotate_by(coef, cosine, sine):
    real_part = coef[:64]
    imag_part = coef[64:]
    return jnp.concatenate(
        [cosine * real_part - sine * imag_part, sine * real_part + cosine * imag_part], axis=0
    )


def image_kernel(
    bits_ref, partner_ref, own_ref, early_ref, late_ref, two_ref, matrix_ref, pixel_ref, out_ref
):
    high_bit = bits_ref[1]
    matrix = stacked_halves(matrix_ref[1 - high_bit, high_bit])
    pixel = stacked_halves(pixel_ref[...])
    early = early_ref.shape[0]
    seconds = {}
    images = {}
    begin = pl.program_id(0) * IMAGE_STEP
    for k in range(IMAGE_STEP + 2):
        if k < IMAGE_STEP:
            box = begin + k
            phase = jnp.where(
                box < early,
                early_ref[jnp.minimum(box, early - 1)],
                late_ref[jnp.maximum(box - early, 0)],
            )
            first = rotate(partner_ref[box], phase)
            seconds[k] = own_ref[box] + product_128(matrix, first)
        if 1 <= k <= IMAGE_STEP:
            turned = rotate_by(
                seconds[k - 1], *[two_ref[h, begin + k - 1] for h in range(2)]
            )
            images[k - 1] = product_128(pixel, turned)
        if k >= 2:
            out_ref[k - 2] = images[k - 2]


KEPT = pl.BlockSpec(memory_space=pltpu.VMEM)


def whole(shape):
    return pl.BlockSpec(shape, lambda *_: (0,) * len(shape))


def params(mebibytes=24):
    return pltpu.CompilerParams(vmem_limit_bytes=mebibytes * 1024 * 1024)


def from_quad(value, mask):
    pairs = [(source, source ^ mask) for source in range(lax.axis_size("quad"))]
    return lax.ppermute(value, "quad", pairs)


def body(sample_box, sample_coords, sample_values, level_one, level_two, phase_one, phase_two):
    senders = lax.axis_size("box")
    boxes = phase_one.shape[1]
    targets = phase_one.shape[3]
    early = EARLY
    phase_one = phase_one[0]
    phase_two = phase_two[0]

    early_shape = (early,) + phase_one.shape[1:]
    late_shape = (boxes - early,) + phase_one.shape[1:]
    sample_box = sample_box.reshape(1, -1)
    packed_shape = (senders // 2, 8, 128)
    operands = (sample_box, sample_coords, sample_values, phase_one)
    results = (packed_shape, early_shape, late_shape)
    packed, early_source, late_source = pl.pallas_call(
        pack_kernel,
        grid=(1,),
        in_specs=[whole(v.shape) for v in operands[:3]] + [pl.BlockSpec(memory_space=pl.ANY)],
        out_specs=[whole(packed_shape)] + [pl.BlockSpec(memory_space=pl.ANY)] * 2,
        out_shape=[jax.ShapeDtypeStruct(v, F32) for v in results],
        scratch_shapes=[pltpu.VMEM(phase_one.shape, F32), pltpu.SemaphoreType.DMA((3,))],
        compiler_params=params(60),
        name="pack",
    )(*operands)
    early_phase = from_quad(early_source, 2)
    arrived = lax.all_to_all(
        packed.reshape(senders, 4, 128), "box", split_axis=0, concat_axis=0, tiled=True
    )
    arrived, early_phase = lax.optimization_barrier((arrived, early_phase))
    ordered = pl.pallas_call(
        sort_kernel,
        out_shape=jax.ShapeDtypeStruct((BLOCKS + 1, 8, 2 * TILE), F32),
        scratch_shapes=[pltpu.VMEM((8, senders * SLOTS), F32)],
        compiler_params=params(),
        name="sort",
    )(arrived.reshape(senders // 2, 8, 128))
    others = [from_quad(ordered, mask) for mask in (1, 2, 3)]

    quad_index = lax.axis_index("quad")
    bits = jnp.stack([quad_index % 2, quad_index // 2])

    turn_in = pl.BlockSpec((4,) + phase_one.shape[1:], lambda b: (b, 0, 0))
    turn_out = pl.BlockSpec((2, 4) + phase_one.shape[1:], lambda b: (0, b, 0, 0))
    turn_one, turn_two = pl.pallas_call(
        turn_kernel,
        grid=(boxes // 4,),
        in_specs=[turn_in] * 2,
        out_specs=[turn_out] * 2,
        out_shape=[jax.ShapeDtypeStruct((2,) + phase_one.shape, F32)] * 2,
        compiler_params=params(60),
        name="turn",
    )(phase_one, phase_two)

    scalars = pl.BlockSpec(memory_space=pltpu.SMEM)
    token = pl.pallas_call(
        token_kernel,
        in_specs=[KEPT],
        out_specs=KEPT,
        out_shape=jax.ShapeDtypeStruct((8, 128), F32),
        compiler_params=params(),
        name="token",
    )(ordered)
    late_source, token = lax.optimization_barrier((late_source, token))
    own_leaf = pl.pallas_call(
        own_leaf_kernel,
        in_specs=[KEPT] * 2,
        out_specs=KEPT,
        out_shape=jax.ShapeDtypeStruct((1, boxes + 1, 512, 128), F32),
        scratch_shapes=leaf_scratch(1),
        compiler_params=params(24),
        cost_estimate=pl.CostEstimate(flops=9 * 10**9, bytes_accessed=8 * 10**6, transcendentals=0),
        name="own_leaf",
    )(ordered, token)
    late_phase = from_quad(late_source, 2)
    partner, own = pl.pallas_call(
        leaf_kernel,
        in_specs=[scalars] + [KEPT] * 7,
        out_specs=[KEPT] * 2,
        out_shape=[jax.ShapeDtypeStruct((boxes, 128, targets), F32)] * 2,
        scratch_shapes=[pltpu.VMEM((3, boxes + 1, 512, 128), F32)] + leaf_scratch(3),
        compiler_params=params(32),
        cost_estimate=pl.CostEstimate(flops=30 * 10**9, bytes_accessed=24 * 10**6, transcendentals=0),
        name="leaf",
    )(bits, *others, own_leaf, level_one, level_two, turn_one)

    pixel = jnp.asarray(pixel_matrix())

    image = pl.pallas_call(
        image_kernel,
        grid=(boxes // IMAGE_STEP,),
        in_specs=[scalars] + [KEPT] * 7,
        out_specs=pl.BlockSpec((IMAGE_STEP, 128, targets), lambda b: (b, 0, 0)),
        out_shape=jax.ShapeDtypeStruct((boxes, 128, targets), F32),
        compiler_params=params(24),
        name="image",
    )(bits, partner, own, early_phase, late_phase, turn_two, level_two, pixel)
    return image[None]


def solution(mesh):
    placed = (
        P(("quad", "box")),
        P(None, ("quad", "box")),
        P(None, ("quad", "box")),
        P(),
        P(),
        P("quad", "box", None, None),
        P("quad", "box", None, None),
    )
    return jax.shard_map(
        body, mesh=mesh, in_specs=placed, out_specs=P("quad", "box", None, None), check_vma=False
    )
```
